32 devices in a mesh: expert: 8 (over y, x, core), dp: 4 (over z).
Axes of the slice: x: 2, y: 2, z: 4, core: 2. Of those that a mesh axis runs over, the one named last changes fastest.
Arguments:
- dy_values: bfloat16 [2048, 4096], P('expert', 'dp'), may hold values from -6 to 6
- dy_scales: bfloat16 [2048, 32], P('expert', 'dp'), may hold values from 0.25 to 4
- expert_ids: int32 [2048, 1], P('expert'), may hold values from 0 to 7; in each aligned block of 256 rows (0 to 255, 256 to 511, ...) at most 64 rows name the same one
- saved_pre: bfloat16 [4096, 2048], P('expert'), may hold values from -6 to 6
- w_gate: bfloat16 [8, 4096, 1024], P('expert', 'dp'), may hold values from -0.1875 to 0.1875
- w_up: bfloat16 [8, 4096, 1024], P('expert', 'dp'), may hold values from -0.1875 to 0.1875
- w_down: bfloat16 [8, 4096, 1024], P('expert', 'dp'), may hold values from -0.09375 to 0.09375
Outputs:
- grad_input: bfloat16 [2048, 4096], P('expert', 'dp')
- grad_down: float32 [8, 4096, 1024], P('expert', 'dp')
The draws below stay inside these ranges and needn't reach their ends.
Inputs may be any that keep to these rules, and one draw needn't show every extreme that they name: `expert_ids`: among the rows of one index of expert (aligned blocks of 256 rows) no expert occurs more than 64 times.
All inputs are finite; a program needn't handle non-finite values.
Results may differ from the reference program's by a relative error of at most 0.0057.
Values may be sent and summed in bfloat16 or wider, within the bound.
No kernel may reach another device: no remote copies, remote signals or barrier semaphores. Data moves between devices by JAX's collectives and lax.ppermute only.
A program may use at most 64 MiB of HBM per device.

```python
import math
import jax
import jax.numpy as jnp
import numpy as np
from jax import lax

D = 4096
FF = 1024
BLOCK = 128
ROWS_DEV = 256
SLOTS = 512
EXPERTS = 8
CAP = 64
ROWS = 2048
SLOT_ROWS = 4096


def steps_of(rng, dims, shards, smallest, high):
    loudness, own = 1.0, jax.random.fold_in(rng, 6)
    for dim, blocks in shards:
        draws = jnp.exp(jax.random.uniform(jax.random.fold_in(own, dim), (blocks,), jnp.float32, smallest / len(shards), high / len(shards)))
        loudness = loudness * jnp.repeat(draws, dims[dim] // blocks).reshape([-1 if axis == dim else 1 for axis in range(len(dims))])
    return loudness


def routed_block(key, own, number, rows, amount, top, limit, lean):
    sequence = jax.random.permutation(key, amount)
    packed, ordinary = shares(amount, rows * top, limit, lean, True), shares(amount, rows * top, limit, lean, False)
    places = jnp.arange(amount)

    def named(tallies, offset_by):
        used = int((tallies > 0).sum())
        fixed = max(1, used // 4)
        shifted = fixed + (places - fixed + offset_by * (used - fixed)) % max(1, amount - fixed)
        return jnp.zeros((amount,), jnp.int32).at[sequence[jnp.where(places < fixed, places, shifted)]].set(jnp.asarray(tallies, jnp.int32))

    tallies = jnp.where(number % 4 == 0, named(packed, number // 4), named(ordinary, number - number // 4 - 1))
    mixed = jax.random.permutation(jax.random.fold_in(own, 3), amount)
    source_of, receiver = mixed[0:amount // 2 * 2:2], mixed[1:amount // 2 * 2:2]
    margin = jnp.minimum(tallies[source_of] - 1, limit - tallies[receiver]) // 2
    margin = jnp.where((source_of == sequence[0]) | (receiver == sequence[0]) | (tallies[receiver] == 0), 0, jnp.maximum(margin, 0))
    shifted = jax.random.randint(jax.random.fold_in(own, 4), (amount // 2,), 0, 1 << 20) % (margin + 1)
    tallies = tallies.at[source_of].add(-shifted).at[receiver].add(shifted)
    items = jnp.searchsorted(jnp.cumsum(tallies), jnp.arange(rows * top), side="right").astype(jnp.int32)
    table = items.reshape(top, rows).T
    table = table[jax.random.permutation(jax.random.fold_in(own, 1), rows)]
    offset_by = jax.random.randint(jax.random.fold_in(own, 2), (rows, 1), 0, top)
    return jnp.take_along_axis(table, (jnp.arange(top)[None, :] + offset_by) % top, axis=1)


def shares(number_of, total, reach, slope, full):
    weights = [(1 << 20) // math.isqrt(standing ** slope) + 1 for standing in range(1, number_of + 1)]
    largest = reach if full else min(reach, max(-(-total // number_of), total * weights[0] // sum(weights)))
    least = 1 if total - largest >= number_of - 1 else 0
    holding, surplus = [largest] + [least] * (number_of - 1), total - largest - least * (number_of - 1)
    while surplus > 0:
        movable = [i for i in range(1, number_of) if holding[i] < largest] or [i for i in range(1, number_of) if holding[i] < reach]
        mass, budget = sum([weights[i] for i in movable]), surplus
        for i in movable:
            extra = min(reach - holding[i], max(1, budget * weights[i] // mass), surplus)
            holding[i] = holding[i] + extra
            surplus = surplus - extra
    return np.array(holding)


def scatter_about(rng, shape, scale, limit, pieces=(), held_as=jnp.bfloat16):
    result = jax.random.normal(rng, shape, jnp.float32) * scale
    if len(pieces) > 0:
        result = steps_of(rng, shape, pieces, -0.22, 0.18) * result
    return jnp.clip(result, min=-limit, max=limit).astype(held_as)


def setup_inputs(seed: int = 0) -> dict:
    seeds = jax.random.split(jax.random.key(seed), 8)
    dy_values = scatter_about(seeds[0], (ROWS, D), 1.0, 6.0, ((0, 8), (1, 4)))
    dy_scales = jnp.clip(jnp.exp(math.log(4.0) - 2.7725887 * jax.random.uniform(seeds[1], (ROWS, D // BLOCK), jnp.float32) ** steps_of(seeds[1], (ROWS, D // BLOCK), ((0, 8), (1, 4)), -0.2, 0.2)), 0.25, 4.0).astype(jnp.bfloat16)
    expert_ids_keys = jax.random.split(jax.random.fold_in(seeds[2], 1), ROWS // ROWS_DEV)
    expert_ids_turns = jax.random.permutation(jax.random.fold_in(seeds[2], 3), ROWS // ROWS_DEV)
    expert_ids = jax.vmap(lambda own, number: routed_block(jax.random.fold_in(seeds[2], 2), own, number, ROWS_DEV, EXPERTS, 1, CAP, 2))(expert_ids_keys, expert_ids_turns).reshape((ROWS, 1))
    saved_pre = scatter_about(seeds[3], (SLOT_ROWS, 2 * FF), 1.0, 6.0, ((0, 8),))
    w_gate = scatter_about(seeds[4], (EXPERTS, D, FF), FF ** -0.5, 0.1875, ((0, 8), (1, 4)))
    w_up = scatter_about(seeds[5], (EXPERTS, D, FF), FF ** -0.5, 0.1875, ((0, 8), (1, 4)))
    w_down = scatter_about(seeds[6], (EXPERTS, D, FF), D ** -0.5, 0.09375, ((0, 8), (1, 4)))
    return {"dy_values": dy_values, "dy_scales": dy_scales, "expert_ids": expert_ids, "saved_pre": saved_pre, "w_gate": w_gate, "w_up": w_up, "w_down": w_down}


def dequantize(values, scales):
    row_count, feature_count = values.shape
    block_count = scales.shape[1]
    blocked = values.astype(jnp.float32).reshape(row_count, block_count, feature_count // block_count)
    blocked = blocked * scales.astype(jnp.float32)[:, :, None]
    return blocked.reshape(row_count, feature_count).astype(jnp.bfloat16)


def swiglu_back(hidden_grad, gate_pre, up_pre):
    sigmoid_gate = jax.nn.sigmoid(gate_pre)
    d_gate = hidden_grad * up_pre * sigmoid_gate * (1.0 + gate_pre * (1.0 - sigmoid_gate))
    d_up = hidden_grad * jax.nn.silu(gate_pre)
    return jnp.concatenate([d_gate, d_up], axis=1).astype(jnp.bfloat16)


def reference(dy_values, dy_scales, expert_ids, saved_pre, w_gate, w_up, w_down):
    row_total = dy_values.shape[0]
    route_ids = expert_ids[:, 0].astype(jnp.int32)
    per_expert = SLOTS // EXPERTS
    by_source = route_ids.reshape(-1, ROWS_DEV)
    onehot = (by_source[:, :, None] == jnp.arange(EXPERTS, dtype=jnp.int32)[None, None, :]).astype(jnp.int32)
    earlier = jnp.cumsum(onehot, axis=1) - onehot
    rank = jnp.sum(earlier * onehot, axis=2).reshape(-1)
    source = jnp.arange(row_total, dtype=jnp.int32) // ROWS_DEV
    position = (route_ids * SLOTS + source * per_expert + rank).astype(jnp.int32)
    grad_rows = dequantize(dy_values, dy_scales)
    owner = jnp.full((SLOT_ROWS,), row_total, jnp.int32).at[position].set(jnp.arange(row_total, dtype=jnp.int32))
    padded_rows = jnp.concatenate([grad_rows, jnp.zeros((1, D), jnp.bfloat16)], axis=0)

    def one_expert(expert):
        first = (expert * SLOTS).astype(jnp.int32)
        members = lax.dynamic_slice_in_dim(owner, first, SLOTS)
        received = padded_rows[members]
        saved = lax.dynamic_slice_in_dim(saved_pre, first, SLOTS, 0)
        gate_pre = saved[:, :FF].astype(jnp.float32)
        up_pre = saved[:, FF:].astype(jnp.float32)
        hidden = (jax.nn.silu(gate_pre) * up_pre).astype(jnp.bfloat16)
        hidden_grad = jnp.dot(received, w_down[expert], preferred_element_type=jnp.float32)
        pre_grad = swiglu_back(hidden_grad, gate_pre, up_pre)
        paired = jnp.concatenate([w_gate[expert], w_up[expert]], axis=1)
        slot_grad = lax.dot_general(pre_grad, paired, (((1,), (1,)), ((), ())), preferred_element_type=jnp.float32).astype(jnp.bfloat16)
        weight_grad = lax.dot_general(received, hidden, (((0,), (0,)), ((), ())), preferred_element_type=jnp.float32)
        return weight_grad, slot_grad

    grad_down, slot_grads = lax.map(one_expert, jnp.arange(EXPERTS, dtype=jnp.int32))
    grad_input = slot_grads.reshape(SLOT_ROWS, D)[position]
    return grad_input, grad_down
```

```python
import functools

import jax
import jax.numpy as jnp
from jax import lax
from jax.experimental import pallas as pl
from jax.experimental.pallas import tpu as pltpu
from jax.sharding import PartitionSpec as P

CHUNKS = ((0, 1), (6, 7), (3, 5), (2, 4))
EARLY, LATE = sum(CHUNKS[:-1], ()), CHUNKS[-1]
ORDER = (
    ("first", 0), ("prep", 0), ("add", 0), ("first", 1), ("turn", 0), ("add", 0), ("add", 1),
    ("first", 2), ("first", 3), ("second", 0), ("add", 2), ("add", 1), ("add", 3), ("down", 0),
    ("second", 1), ("add", 2), ("add", 3), ("second", 2), ("second", 3),
)
WEIGHT = 20
LATE_WEIGHT = 20
MIB = 1 << 20
BF16, F32 = jnp.bfloat16, jnp.float32
TRANSPOSED = (((1,), (1,)), ((), ()))
BY_ROWS = (((0,), (0,)), ((), ()))


VMEM, SMEM, HBM, ANY = (
    pl.BlockSpec(memory_space=space) for space in (pltpu.VMEM, pltpu.SMEM, pltpu.HBM, pl.ANY)
)


def call(
    body, name, operands, specs, outs, out_specs, work, vmem,
    scratch=(), after=(), passed=(), weight=WEIGHT,
):
    count, results = len(operands), len(outs)
    inputs = count + len(after) + len(passed)

    def run(*refs):
        kept = refs[:count] + refs[inputs : inputs + results]
        body(*kept, *refs[inputs + results + len(passed) :])

    return pl.pallas_call(
        run,
        name=name,
        out_shape=list(outs) + [jax.ShapeDtypeStruct(x.shape, x.dtype) for x in passed],
        in_specs=list(specs) + [ANY] * (len(after) + len(passed)),
        out_specs=list(out_specs) + [ANY] * len(passed),
        scratch_shapes=scratch,
        input_output_aliases={
            count + len(after) + i: results + i for i in range(len(passed))
        },
        compiler_params=pltpu.CompilerParams(vmem_limit_bytes=vmem * MIB),
        cost_estimate=pl.CostEstimate(
            flops=weight * work, bytes_accessed=weight * work // 300, transcendentals=0
        ),
    )(*operands, *after, *passed)


def in_hbm(array):
    return pltpu.with_memory_space_constraint(array, pltpu.HBM)


def swish_parts(pre, width):
    gate, up = pre[:, :width].astype(F32), pre[:, width:].astype(F32)
    sigmoid = jax.nn.sigmoid(gate)
    return gate, up, sigmoid


def tiles(size):
    step = 256 if size % 256 == 0 else size
    return [slice(i, i + step) for i in range(0, size, step)]


def arrays_of(blocks):
    found = []
    for array, _ in blocks:
        if not any(array is other for other in found):
            found.append(array)
    return found


def spots_of(blocks, arrays):
    return [(next(i for i, x in enumerate(arrays) if x is array), row) for array, row in blocks]


def rows_at(refs, spots, cap):
    return jnp.concatenate([refs[i][row : row + cap] for i, row in spots], axis=0)


def pack_body(
    groups, cap, info, scales, ids, values, place, even, odd, ids_in, rows_in, sems
):
    bring_rows = pltpu.make_async_copy(values, rows_in, sems.at[0])
    bring_ids = pltpu.make_async_copy(ids, ids_in, sems.at[1])
    bring_ids.start()
    bring_rows.start()
    rows, features = values.shape
    slots, lines = groups * cap, max(8, groups)
    count = scales.shape[0]
    owner = lax.broadcasted_iota(jnp.int32, (count, features), 1) // (features // count)
    spread = jnp.where(owner == lax.broadcasted_iota(jnp.int32, (count, features), 0), 1.0, 0.0)
    factor = lax.dot_general(
        scales[...].astype(BF16), spread.astype(BF16), BY_ROWS, preferred_element_type=F32
    )
    bring_ids.wait()
    route = ids_in[...]
    line = lax.broadcasted_iota(jnp.int32, (lines, rows), 0)
    onehot = jnp.where(line == route, 1.0, 0.0)
    sooner = lax.broadcasted_iota(jnp.int32, (rows, rows), 0)
    later = lax.broadcasted_iota(jnp.int32, (rows, rows), 1)
    before = jnp.where(sooner < later, 1.0, 0.0).astype(BF16)
    earlier = jnp.dot(onehot.astype(BF16), before, preferred_element_type=F32)
    rank = jnp.sum(earlier * onehot, axis=0, keepdims=True).astype(jnp.int32)
    position = (route ^ info[1]) * cap + rank
    slot = lax.broadcasted_iota(jnp.int32, (slots, rows), 0)
    chosen = jnp.where(slot == position, 1.0, 0.0).astype(BF16)
    place[...] = chosen
    bring_rows.wait()
    scaled = (rows_in[...].astype(F32) * factor).astype(BF16)
    for part in tiles(features):
        packed = jnp.dot(chosen, scaled[:, part], preferred_element_type=F32).astype(BF16)
        for k in range(groups):
            out = odd if k % 2 else even
            out[k // 2 * cap : (k // 2 + 1) * cap, part] = packed[k * cap : (k + 1) * cap]


def pack(info, ids, values, scales, groups, cap):
    rows, features = values.shape
    half = jax.ShapeDtypeStruct((groups // 2 * cap, features), BF16)
    return call(
        functools.partial(pack_body, groups, cap),
        "pack",
        (info, scales.T.astype(F32), in_hbm(ids.T), in_hbm(values)),
        (SMEM, VMEM, HBM, HBM),
        [jax.ShapeDtypeStruct((groups * cap, rows), BF16), half, half],
        [VMEM] * 3,
        2 * rows * groups * cap * features,
        24,
        [
            pltpu.VMEM((1, rows), jnp.int32),
            pltpu.VMEM((rows, features), BF16),
            pltpu.SemaphoreType.DMA((2,)),
        ],
    )


def first_body(count, spots, bundles, cap, info, weight, *refs):
    arrays, send, keep = refs[:count], refs[count], refs[count + 1]
    for bundle, out in zip(bundles, refs[count + 2 :]):
        out[...] = rows_at(arrays, bundle, cap)
    half = len(spots) // 2
    upper, lower = rows_at(arrays, spots[:half], cap), rows_at(arrays, spots[half:], cap)
    odd = info[0] == 1
    rows = jnp.concatenate([jnp.where(odd, upper, lower), jnp.where(odd, lower, upper)], axis=0)
    for part in tiles(weight.shape[1]):
        partial = jnp.dot(rows, weight[:, part], preferred_element_type=F32)
        send[:, part] = partial[: half * cap].astype(BF16)
        keep[:, part] = partial[half * cap :]


def first(info, blocks, weight, cap, after, bundles=()):
    arrays = arrays_of([block for group in (blocks, *bundles) for block in group])
    features, width = weight.shape
    size = len(blocks) // 2 * cap
    return call(
        functools.partial(
            first_body,
            len(arrays),
            spots_of(blocks, arrays),
            [spots_of(bundle, arrays) for bundle in bundles],
            cap,
        ),
        "first",
        (info, weight, *arrays),
        [SMEM] + [VMEM] * (1 + len(arrays)),
        [jax.ShapeDtypeStruct((size, width), BF16), jax.ShapeDtypeStruct((size, width), F32)]
        + [jax.ShapeDtypeStruct((len(bundle) * cap, features), BF16) for bundle in bundles],
        [VMEM] * (2 + len(bundles)),
        4 * size * features * width,
        16,
        after=after,
    )


def add_body(count, keep, *refs):
    total = keep[...]
    for got in refs[:count]:
        total = total + got[...].astype(F32)
    refs[count][...] = total.astype(BF16)


def add(keep, gots, after):
    return call(
        functools.partial(add_body, len(gots)),
        "add",
        (keep, *gots),
        [VMEM] * (1 + len(gots)),
        [jax.ShapeDtypeStruct(keep.shape, BF16)],
        [VMEM],
        keep.size,
        8,
        after=after,
    )[0]


def prep_body(saved, gate_factor, up_factor, hidden):
    slots, width = hidden.shape
    step = 32 if slots % 32 == 0 else slots

    def some(i, carry):
        at = pl.ds(pl.multiple_of(i * step, step), step)
        gate, up, sigmoid = swish_parts(saved[at, :], width)
        silu = gate * sigmoid
        gate_factor[at, :] = up * sigmoid * (1.0 + gate * (1.0 - sigmoid))
        up_factor[at, :] = silu
        hidden[at, :] = (silu * up).astype(BF16)
        return carry

    lax.fori_loop(0, slots // step, some, 0)


def prep(saved_pre, after):
    slots, width = saved_pre.shape[0], saved_pre.shape[1] // 2
    return call(
        prep_body,
        "prep",
        (saved_pre,),
        [VMEM],
        [jax.ShapeDtypeStruct((slots, width), dtype) for dtype in (F32, F32, BF16)],
        [VMEM] * 3,
        1,
        16,
        after=after,
    )


def turn_body(*refs):
    half = len(refs) // 2
    for weight, turned in zip(refs[:half], refs[half:]):
        for part in tiles(weight.shape[0]):
            turned[:, part] = weight[part, :].T


def turn(weights, after):
    shapes = [jax.ShapeDtypeStruct(x.shape[::-1], x.dtype) for x in weights]
    count = len(weights)
    return call(
        turn_body, "turn", weights, [VMEM] * count, shapes, [VMEM] * count, 1, 16, after=after
    )


def slots_of(ref, info, k, cap):
    return ref[pl.ds(pl.multiple_of((info[1] ^ k) * cap, cap), cap), :]


def second_body(chunk, info, own, other, gate_factor, up_factor, w_gate, w_up, *outs):
    cap = outs[0].shape[0]
    odd = info[0] == 1
    mine, yours = own[...], other[...]
    grad = jnp.concatenate([jnp.where(odd, yours, mine), jnp.where(odd, mine, yours)], axis=0)
    grad = grad.astype(F32)
    d_gate, d_up = (
        jnp.concatenate(
            [
                grad[i * cap : (i + 1) * cap] * slots_of(factor, info, k, cap)
                for i, k in enumerate(chunk)
            ],
            axis=0,
        ).astype(BF16)
        for factor in (gate_factor, up_factor)
    )
    for part in tiles(w_gate.shape[1]):
        result = jnp.dot(d_gate, w_gate[:, part], preferred_element_type=F32)
        result += jnp.dot(d_up, w_up[:, part], preferred_element_type=F32)
        result = result.astype(BF16)
        for i, out in enumerate(outs):
            out[:, part] = result[i * cap : (i + 1) * cap]


def second(info, own, other, factors, weights, chunk, cap, after):
    width, features = weights[0].shape
    return call(
        functools.partial(second_body, chunk),
        "second",
        (info, own, other, *factors, *weights),
        [SMEM] + [VMEM] * 6,
        [jax.ShapeDtypeStruct((cap, features), BF16)] * len(chunk),
        [VMEM] * len(chunk),
        4 * len(chunk) * cap * features * width,
        24,
        after=after,
        weight=LATE_WEIGHT,
    )


def down_body(count, spots, groups, info, place, hidden, *refs):
    arrays, out, early, late, sums, sems = refs[:count], *refs[count:]
    cap = hidden.shape[0] // len(spots)
    features, width = out.shape
    for group, turned in zip(groups, (early, late)):
        turned[...] = rows_at([place], [(0, k * cap) for k in group], cap).T
    mine = jnp.concatenate([slots_of(hidden, info, k, cap) for k in range(len(spots))], axis=0)
    tile = sums.shape[1]
    copies = []
    for i in range(features // tile):
        part = [arrays[a][row : row + cap, i * tile : (i + 1) * tile] for a, row in spots]
        part = jnp.concatenate(part, axis=0)
        sums[i] = lax.dot_general(part, mine, BY_ROWS, preferred_element_type=F32)
        copies.append(
            pltpu.make_async_copy(sums.at[i], out.at[pl.ds(i * tile, tile)], sems.at[i])
        )
        copies[-1].start()
    for copy in copies:
        copy.wait()


def down(info, blocks, hidden, place, features, groups, after):
    arrays = arrays_of(blocks)
    slots, width = hidden.shape
    tile = min(features, 256)
    steps = features // tile
    return call(
        functools.partial(down_body, len(arrays), spots_of(blocks, arrays), groups),
        "down",
        (info, place, hidden, *arrays),
        [SMEM] + [VMEM] * (2 + len(arrays)),
        [jax.ShapeDtypeStruct((features, width), F32)]
        + [
            jax.ShapeDtypeStruct((place.shape[1], slots // len(blocks) * len(group)), BF16)
            for group in groups
        ],
        [HBM, VMEM, VMEM],
        2 * slots * features * width,
        24,
        [pltpu.VMEM((steps, tile, width), F32), pltpu.SemaphoreType.DMA((steps,))],
        after=after,
        weight=LATE_WEIGHT,
    )


def gather_body(count, place, *refs):
    blocks, sooner, out = refs[:count], refs[count:-1], refs[-1]
    for part in tiles(out.shape[1]):
        returned = jnp.concatenate([block[:, part] for block in blocks], axis=0)
        rows = jnp.dot(place[...], returned, preferred_element_type=F32).astype(BF16)
        out[:, part] = rows + sooner[0][:, part] if sooner else rows


def gather(place, blocks, after, sooner=()):
    count, (cap, features) = len(blocks), blocks[0].shape
    rows = place.shape[0]
    return call(
        functools.partial(gather_body, count),
        "gather",
        (place, *blocks, *sooner),
        [VMEM] * (1 + count + len(sooner)),
        [jax.ShapeDtypeStruct((rows, features), BF16)],
        [VMEM],
        2 * rows * count * cap * features,
        16,
        after=after,
    )[0]


def swap(block, axis, k):
    size = lax.axis_size(axis)
    return lax.ppermute(block, axis, [(i, i ^ k) for i in range(size)])


def near_device(dy_values, dy_scales, expert_ids, saved_pre, w_gate, w_up, w_down):
    groups = lax.axis_size("expert")
    cap = saved_pre.shape[0] // groups
    features = dy_values.shape[1]
    info = jnp.stack([lax.axis_index("dp") % 2, lax.axis_index("expert")]).astype(jnp.int32)
    place, even, odd = pack(info, expert_ids, dy_values, dy_scales, groups, cap)
    last, result = [place], {}
    keeps, gots, owns, others, returned = {}, {}, {}, {}, {}

    side = swap(odd, "expert", 1)
    blocks = {0: (even, 0), 1: (side, 0)}
    chips = range(2, groups, 2)
    bundles = [((even, k // 2 * cap), (side, k // 2 * cap)) for k in chips]

    def do_first(c):
        chosen = [blocks[k] for k in CHUNKS[c]]
        send, keeps[c], *sent = first(info, chosen, w_down[0], cap, last, () if c else bundles)
        last[:] = [send]
        gots[c] = [swap(send, "dp", 1)]
        for k, bundle in sorted(zip(chips, sent), reverse=True):
            got = swap(bundle, "expert", k)
            blocks.update({k: (got, 0), k + 1: (got, cap)})

    def do_add(c):
        part = add(keeps[c], gots[c], last)
        last[:] = [part]
        if len(gots[c]) == 1:
            gots[c].append(swap(part, "dp", 2))
        else:
            owns[c], others[c] = part, swap(part, "dp", 1)

    def do_prep(_):
        *result["factors"], result["hidden"] = prep(saved_pre, last)
        last[:] = [result["hidden"]]

    def do_turn(_):
        result["weights"] = turn((w_gate[0], w_up[0]), last)
        last[:] = result["weights"][:1]

    def do_second(c):
        grads = second(
            info, owns[c], others[c], result["factors"], result["weights"], CHUNKS[c], cap, last
        )
        last[:] = [grads[0]]
        for k, grad in zip(CHUNKS[c], grads):
            returned[k] = swap(grad, "expert", k) if k else grad

    def do_down(_):
        every = [blocks[k] for k in range(groups)]
        result["down"], *result["turned"] = down(
            info, every, result["hidden"], place, features, (EARLY, LATE), last
        )
        last[:] = result["turned"][:1]

    steps = {
        "first": do_first,
        "add": do_add,
        "prep": do_prep,
        "turn": do_turn,
        "second": do_second,
        "down": do_down,
    }
    for step, c in ORDER:
        steps[step](c)
    early, late = result["turned"]
    sooner = gather(early, [returned[k] for k in EARLY], last)
    grad_input = gather(late, [returned[k] for k in LATE], [], [sooner])
    return (grad_input, result["down"][None])


def far_device(dy_values, dy_scales, expert_ids, saved_pre, w_gate, w_up, w_down):
    groups, width = lax.axis_size("expert"), w_down.shape[2]
    slots = saved_pre.shape[0]
    cap = slots // groups
    route = expert_ids[:, 0]
    rows, count = route.shape[0], dy_scales.shape[1]
    onehot = (route[:, None] == jnp.arange(groups, dtype=jnp.int32)[None, :]).astype(BF16)
    earlier = jnp.dot(jnp.tri(rows, k=-1, dtype=BF16), onehot, preferred_element_type=F32)
    rank = jnp.sum(earlier * onehot.astype(F32), axis=1).astype(jnp.int32)
    place = route * cap + rank
    chosen = (place[:, None] == jnp.arange(slots, dtype=jnp.int32)[None, :]).astype(BF16)
    scaled = dy_values.astype(F32).reshape(rows, count, -1) * dy_scales.astype(F32)[:, :, None]
    scaled = scaled.reshape(dy_values.shape).astype(BF16)
    packed = lax.dot_general(chosen, scaled, BY_ROWS, preferred_element_type=F32).astype(BF16)
    received = lax.all_to_all(packed, "expert", split_axis=0, concat_axis=0, tiled=True)
    gate, up, sigmoid = swish_parts(saved_pre, width)
    hidden = (gate * sigmoid * up).astype(BF16)
    partial = jnp.dot(received, w_down[0], preferred_element_type=F32)
    grad = lax.psum(partial, "dp")
    d_gate = (grad * up * sigmoid * (1.0 + gate * (1.0 - sigmoid))).astype(BF16)
    d_up = (grad * (gate * sigmoid)).astype(BF16)
    result = lax.dot_general(d_gate, w_gate[0], TRANSPOSED, preferred_element_type=F32)
    result += lax.dot_general(d_up, w_up[0], TRANSPOSED, preferred_element_type=F32)
    returned = lax.all_to_all(
        result.astype(BF16), "expert", split_axis=0, concat_axis=0, tiled=True
    )
    grad_input = jnp.dot(chosen, returned, preferred_element_type=F32).astype(BF16)
    grad_down = lax.dot_general(received, hidden, BY_ROWS, preferred_element_type=F32)
    return (grad_input, grad_down[None])


def solution(mesh):
    near = mesh.shape["expert"] == 8 and mesh.shape["dp"] == 4
    return jax.shard_map(
        near_device if near else far_device,
        mesh=mesh,
        in_specs=(
            P("expert", "dp"),
            P("expert", "dp"),
            P("expert", None),
            P("expert", None),
            P("expert", "dp", None),
            P("expert", "dp", None),
            P("expert", "dp", None),
        ),
        out_specs=(P("expert", "dp"), P("expert", "dp", None)),
        check_vma=False,
    )
```

```python
import functools

import jax
import jax.numpy as jnp
from jax import lax
from jax.experimental import pallas as pl
from jax.experimental.pallas import tpu as pltpu
from jax.sharding import PartitionSpec as P

CHUNKS = ((0, 1), (6, 7), (2, 4), (3, 5))
LATER = (2, 4, 3, 5, 0)
PARTS = (CHUNKS[2], CHUNKS[0] + CHUNKS[1], CHUNKS[3])
ORDER = (
    ("first", 0), ("diagonal", 0), ("add", 0), ("prep", 0), ("turn", 0), ("first", 1),
    ("first", 2), ("add", 0), ("add", 1), ("first", 3), ("add", 2), ("add", 1), ("down", 0),
    ("add", 3), ("release", 0), ("add", 2), ("second", 1), ("add", 3), ("second", 0),
    ("second", 2), ("cross", 0), ("second", 3), ("gather", 0), ("gather", 1),
)
HELD = (0,)
COST = {
    "place": 10**10, "pack": 10**10, "rest": 1, "first": 1, "prep": 1, "turn": 1,
    "add": 10**9, "release": 1, "pair": 1, "second": 10**10, "down": 1, "gather": 1, "finish": 1,
}
MIB = 1 << 20
BF16, F32 = jnp.bfloat16, jnp.float32
TRANSPOSED = (((1,), (1,)), ((), ()))
BY_ROWS = (((0,), (0,)), ((), ()))


VMEM, HBM, ANY = (
    pl.BlockSpec(memory_space=space) for space in (pltpu.VMEM, pltpu.HBM, pl.ANY)
)


def call(body, name, operands, specs, outs, out_specs, vmem=16, scratch=(), after=()):
    count, waits = len(operands), len(after)

    def run(*refs):
        body(*refs[:count], *refs[count + waits :])

    return pl.pallas_call(
        run,
        name=name,
        out_shape=outs,
        in_specs=list(specs) + [ANY] * waits,
        out_specs=out_specs,
        scratch_shapes=scratch,
        compiler_params=pltpu.CompilerParams(vmem_limit_bytes=vmem * MIB),
        cost_estimate=pl.CostEstimate(flops=COST[name], bytes_accessed=0, transcendentals=0),
    )(*operands, *after)


def in_hbm(array):
    return pltpu.with_memory_space_constraint(array, pltpu.HBM)


def swish_parts(pre, width):
    gate, up = pre[:, :width].astype(F32), pre[:, width:].astype(F32)
    sigmoid = jax.nn.sigmoid(gate)
    return gate, up, sigmoid


def tiles(size):
    step = 256 if size % 256 == 0 else size
    return [slice(i, i + step) for i in range(0, size, step)]


def arrays_of(blocks):
    found = []
    for array, _ in blocks:
        if not any(array is other for other in found):
            found.append(array)
    return found


def spots_of(blocks, arrays):
    return [(next(i for i, x in enumerate(arrays) if x is array), row) for array, row in blocks]


def rows_at(refs, spots, cap):
    return jnp.concatenate([refs[i][row : row + cap] for i, row in spots], axis=0)


def place_body(groups, cap, ids, place, ids_in, sems):
    bring = pltpu.make_async_copy(ids, ids_in, sems.at[0])
    bring.start()
    rows, slots, lines = ids.shape[1], groups * cap, max(8, groups)
    line = lax.broadcasted_iota(jnp.int32, (lines, rows), 0)
    sooner = lax.broadcasted_iota(jnp.int32, (rows, rows), 0)
    later = lax.broadcasted_iota(jnp.int32, (rows, rows), 1)
    before = jnp.where(sooner < later, 1.0, 0.0).astype(BF16)
    bring.wait()
    route = ids_in[...]
    onehot = jnp.where(line == route, 1.0, 0.0)
    earlier = jnp.dot(onehot.astype(BF16), before, preferred_element_type=F32)
    rank = jnp.sum(earlier * onehot, axis=0, keepdims=True).astype(jnp.int32)
    position = (route ^ lax.axis_index("expert")) * cap + rank
    slot = lax.broadcasted_iota(jnp.int32, (slots, rows), 0)
    place[...] = jnp.where(slot == position, 1.0, 0.0).astype(BF16)


def find_place(ids, groups, cap):
    rows = ids.shape[0]
    return call(
        functools.partial(place_body, groups, cap),
        "place",
        (in_hbm(ids.T),),
        (HBM,),
        [jax.ShapeDtypeStruct((groups * cap, rows), BF16)],
        [VMEM],
        16,
        [pltpu.VMEM((1, rows), jnp.int32), pltpu.SemaphoreType.DMA((1,))],
    )[0]


def put_blocks(place, rows, outs, groups, cap):
    chosen = rows_at([place], [(0, k * cap) for group in groups for k in group], cap)
    for part in tiles(rows.shape[1]):
        packed = jnp.dot(chosen, rows[:, part], preferred_element_type=F32).astype(BF16)
        start = 0
        for group, out in zip(groups, outs):
            out[:, part] = packed[start : start + len(group) * cap]
            start += len(group) * cap


def pack_body(groups, cap, place, scales, values, scaled, *outs):
    features, count = values.shape[1], scales.shape[0]
    owner = lax.broadcasted_iota(jnp.int32, (count, features), 1) // (features // count)
    spread = jnp.where(owner == lax.broadcasted_iota(jnp.int32, (count, features), 0), 1.0, 0.0)
    spread = spread.astype(BF16)
    for part in tiles(features):
        factor = lax.dot_general(
            scales[...], spread[:, part], BY_ROWS, preferred_element_type=F32
        )
        scaled[:, part] = (values[:, part].astype(F32) * factor).astype(BF16)
    put_blocks(place, scaled, outs, groups, cap)


def rest_body(groups, cap, place, scaled, *outs):
    put_blocks(place, scaled, outs, groups, cap)


def pack(place, values, scales, groups, cap):
    rows, features = values.shape
    return call(
        functools.partial(pack_body, groups, cap),
        "pack",
        (place, scales.T, values),
        [VMEM] * 3,
        [jax.ShapeDtypeStruct((rows, features), BF16)]
        + [jax.ShapeDtypeStruct((len(group) * cap, features), BF16) for group in groups],
        [VMEM] * (1 + len(groups)),
    )


def pack_rest(place, scaled, groups, cap, after):
    features = scaled.shape[1]
    return call(
        functools.partial(rest_body, groups, cap),
        "rest",
        (place, scaled),
        [VMEM] * 2,
        [jax.ShapeDtypeStruct((len(group) * cap, features), BF16) for group in groups],
        [VMEM] * len(groups),
        after=after,
    )


def pair_body(count, spots, cap, *refs):
    refs[count][...] = rows_at(refs[:count], spots, cap)


def pair(blocks, cap, after):
    arrays = arrays_of(blocks)
    shape = jax.ShapeDtypeStruct((len(blocks) * cap, arrays[0].shape[1]), BF16)
    return call(
        functools.partial(pair_body, len(arrays), spots_of(blocks, arrays), cap),
        "pair",
        arrays,
        [VMEM] * len(arrays),
        [shape],
        [VMEM],
        after=after,
    )[0]


def first_body(count, spots, cap, weight, *refs):
    arrays, send, keep, both = refs[:count], *refs[count:]
    rows = rows_at(arrays, spots, cap)
    width = weight.shape[1]
    for part in tiles(width):
        both[:, part] = jnp.dot(rows, weight[:, part], preferred_element_type=F32)
    halves = [slice(0, width // 2), slice(width // 2, width)]
    for odd, (theirs, mine) in enumerate((reversed(halves), halves)):

        @pl.when(lax.axis_index("dp") % 2 == odd)
        def _():
            send[...] = both[:, theirs].astype(BF16)
            keep[...] = both[:, mine]


def first(blocks, weight, cap, after):
    arrays = arrays_of(blocks)
    features, width = weight.shape
    size = len(blocks) * cap
    return call(
        functools.partial(first_body, len(arrays), spots_of(blocks, arrays), cap),
        "first",
        (weight, *arrays),
        [VMEM] * (1 + len(arrays)),
        [jax.ShapeDtypeStruct((size, width // 2), dtype) for dtype in (BF16, F32)],
        [VMEM] * 2,
        16,
        [pltpu.VMEM((size, width), F32)],
        after=after,
    )


def add_body(count, keep, *refs):
    total = keep[...]
    for got in refs[:count]:
        total = total + got[...].astype(F32)
    refs[count][...] = total.astype(BF16)


def add(keep, gots, after):
    return call(
        functools.partial(add_body, len(gots)),
        "add",
        (keep, *gots),
        [VMEM] * (1 + len(gots)),
        [jax.ShapeDtypeStruct(keep.shape, BF16)],
        [VMEM],
        16,
        after=after,
    )[0]


def release_body(total, out):
    out[...] = total[...]


def release(total, after):
    shape = jax.ShapeDtypeStruct(total.shape, total.dtype)
    return call(release_body, "release", (total,), [VMEM], [shape], [VMEM], after=after)[0]


def prep_body(saved, gate_factor, up_factor, hidden):
    slots, width = hidden.shape
    step = 32 if slots % 32 == 0 else slots

    def some(i, carry):
        at = pl.ds(pl.multiple_of(i * step, step), step)
        gate, up, sigmoid = swish_parts(saved[at, :], width)
        silu = gate * sigmoid
        gate_factor[at, :] = up * sigmoid * (1.0 + gate * (1.0 - sigmoid))
        up_factor[at, :] = silu
        hidden[at, :] = (silu * up).astype(BF16)
        return carry

    lax.fori_loop(0, slots // step, some, 0)


def prep(saved_pre, after):
    slots, width = saved_pre.shape[0], saved_pre.shape[1] // 2
    return call(
        prep_body,
        "prep",
        (saved_pre,),
        [VMEM],
        [jax.ShapeDtypeStruct((slots, width), dtype) for dtype in (F32, F32, BF16)],
        [VMEM] * 3,
        16,
        after=after,
    )


def turn_body(count, cap, groups, place, *refs):
    weights, turned, places = refs[:count], refs[count : 2 * count], refs[2 * count :]
    for weight, out in zip(weights, turned):
        for part in tiles(weight.shape[0]):
            out[:, part] = weight[part, :].T
    for group, out in zip(groups, places):
        out[...] = rows_at([place], [(0, k * cap) for k in group], cap).T


def turn(weights, place, groups, cap, after):
    count, rows = len(weights), place.shape[1]
    return call(
        functools.partial(turn_body, count, cap, groups),
        "turn",
        (place, *weights),
        [VMEM] * (1 + count),
        [jax.ShapeDtypeStruct(x.shape[::-1], x.dtype) for x in weights]
        + [jax.ShapeDtypeStruct((rows, len(group) * cap), BF16) for group in groups],
        [VMEM] * (count + len(groups)),
        16,
        after=after,
    )


def slots_of(ref, k, cap):
    start = pl.multiple_of((lax.axis_index("expert") ^ k) * cap, cap)
    return ref[pl.ds(start, cap), :]


def second_body(chunk, cap, own, other, gate_factor, up_factor, w_gate, w_up, *refs):
    outs, grads = refs[:-1], refs[-1]
    width, features = w_gate.shape
    halves = [slice(0, width // 2), slice(width // 2, width)]
    for odd, (theirs, mine) in enumerate((reversed(halves), halves)):

        @pl.when(lax.axis_index("dp") % 2 == odd)
        def _():
            grads[:, mine] = own[...]
            grads[:, theirs] = other[...]

    grad = grads[...].astype(F32)
    d_gate, d_up = (
        (grad * jnp.concatenate([slots_of(factor, k, cap) for k in chunk], axis=0))
        .astype(BF16)
        for factor in (gate_factor, up_factor)
    )
    for part in tiles(features):
        result = jnp.dot(d_gate, w_gate[:, part], preferred_element_type=F32)
        result += jnp.dot(d_up, w_up[:, part], preferred_element_type=F32)
        result = result.astype(BF16)
        size = result.shape[0] // len(outs)
        for i, out in enumerate(outs):
            out[:, part] = result[i * size : (i + 1) * size]


def second(own, other, factors, weights, chunk, cap, together, after):
    width, features = weights[0].shape
    count = 1 if together else len(chunk)
    size = len(chunk) // count * cap
    return call(
        functools.partial(second_body, chunk, cap),
        "second",
        (own, other, *factors, *weights),
        [VMEM] * 6,
        [jax.ShapeDtypeStruct((size, features), BF16)] * count,
        [VMEM] * count,
        24,
        [pltpu.VMEM((len(chunk) * cap, width), BF16)],
        after=after,
    )


def down_body(count, spots, hidden, *refs):
    arrays, out, flag, sums, sems = refs[:count], *refs[count:]
    flag[...] = jnp.zeros_like(flag)
    cap = hidden.shape[0] // len(spots)
    features, width = out.shape
    mine = jnp.concatenate([slots_of(hidden, k, cap) for k in range(len(spots))], axis=0)
    tile = sums.shape[1]
    copies = []
    for i in range(features // tile):
        part = [arrays[a][row : row + cap, i * tile : (i + 1) * tile] for a, row in spots]
        part = jnp.concatenate(part, axis=0)
        sums[i] = lax.dot_general(part, mine, BY_ROWS, preferred_element_type=F32)
        copies.append(
            pltpu.make_async_copy(sums.at[i], out.at[pl.ds(i * tile, tile)], sems.at[i])
        )
        copies[-1].start()
    for copy in copies:
        copy.wait()


def down(blocks, hidden, features, after):
    arrays = arrays_of(blocks)
    slots, width = hidden.shape
    tile = min(features, 256)
    steps = features // tile
    return call(
        functools.partial(down_body, len(arrays), spots_of(blocks, arrays)),
        "down",
        (hidden, *arrays),
        [VMEM] * (1 + len(arrays)),
        [jax.ShapeDtypeStruct((features, width), F32), jax.ShapeDtypeStruct((8, 128), F32)],
        [HBM, VMEM],
        24,
        [pltpu.VMEM((steps, tile, width), F32), pltpu.SemaphoreType.DMA((steps,))],
        after=after,
    )


def rows_of(place, arrays, spots, cap, part):
    returned = [arrays[i][row : row + cap, part] for i, row in spots]
    returned = jnp.concatenate(returned, axis=0)
    return jnp.dot(place[...], returned, preferred_element_type=F32).astype(BF16)


def gather_body(count, spots, cap, place, *refs):
    arrays, sooner, out = refs[:count], refs[count:-1], refs[-1]
    for part in tiles(out.shape[1]):
        rows = rows_of(place, arrays, spots, cap, part)
        for others in sooner:
            rows += others[:, part]
        out[:, part] = rows


def gather(place, blocks, cap, sooner, after):
    arrays = arrays_of(blocks)
    rows, features = place.shape[0], arrays[0].shape[1]
    return call(
        functools.partial(gather_body, len(arrays), spots_of(blocks, arrays), cap),
        "gather",
        (place, *arrays, *sooner),
        [VMEM] * (1 + len(arrays) + len(sooner)),
        [jax.ShapeDtypeStruct((rows, features), BF16)],
        [VMEM],
        16,
        after=after,
    )[0]


def finish_body(count, spots, cap, place, sooner, *refs):
    arrays, out, whole, sems = refs[:count], *refs[count:]
    copies = []
    for i, part in enumerate(tiles(out.shape[1])):
        whole[:, part] = rows_of(place, arrays, spots, cap, part) + sooner[:, part]
        copies.append(pltpu.make_async_copy(whole.at[:, part], out.at[:, part], sems.at[i]))
        copies[-1].start()
    for copy in copies:
        copy.wait()


def finish(place, blocks, cap, sooner, after):
    arrays, (rows, features) = arrays_of(blocks), sooner.shape
    return call(
        functools.partial(finish_body, len(arrays), spots_of(blocks, arrays), cap),
        "finish",
        (place, sooner, *arrays),
        [VMEM] * (2 + len(arrays)),
        [jax.ShapeDtypeStruct((rows, features), BF16)],
        [HBM],
        16,
        [
            pltpu.VMEM((rows, features), BF16),
            pltpu.SemaphoreType.DMA((len(tiles(features)),)),
        ],
        after=after,
    )[0]


def swap(block, axis, k):
    size = lax.axis_size(axis)
    return lax.ppermute(block, axis, [(i, i ^ k) for i in range(size)])


def near_device(dy_values, dy_scales, expert_ids, saved_pre, w_gate, w_up, w_down):
    groups = lax.axis_size("expert")
    cap = saved_pre.shape[0] // groups
    features = dy_values.shape[1]
    keeps, gots, owns, others, returned, result = {}, {}, {}, {}, {}, {}

    place = find_place(expert_ids, groups, cap)
    last, sooner = [place], []
    scaled, crossing, ahead = pack(place, dy_values, dy_scales, ((1, 7), (6,)), cap)
    side = swap(crossing, "expert", 1)
    rest = pack_rest(place, scaled, [(k,) for k in LATER], cap, [crossing])
    last[:] = rest[-1:]
    blocks = {1: (side, 0)}
    for k, block in zip(LATER, rest):
        blocks[k] = (swap(block, "expert", k) if k else block, 0)

    def do_diagonal(_):
        both = pair([(ahead, 0), (side, cap)], cap, last)
        last[:] = [both]
        got = swap(both, "expert", 6)
        blocks.update({6: (got, 0), 7: (got, cap)})

    def do_first(c):
        send, keeps[c] = first([blocks[k] for k in CHUNKS[c]], w_down[0], cap, last)
        last[:] = [send]
        gots[c] = [swap(send, "dp", 1)]

    def do_add(c):
        part = add(keeps[c], gots[c], last)
        last[:] = [part]
        if len(gots[c]) == 1:
            gots[c].append(swap(part, "dp", 2))
        elif c in HELD:
            owns[c] = part
        else:
            owns[c], others[c] = part, swap(part, "dp", 1)

    def do_release(c):
        owns[c] = release(owns[c], last)
        last[:] = [owns[c]]
        others[c] = swap(owns[c], "dp", 1)

    def do_prep(_):
        *result["factors"], result["hidden"] = prep(saved_pre, last)
        last[:] = [result["hidden"]]

    def do_turn(_):
        turned = turn((w_gate[0], w_up[0]), place, PARTS, cap, last)
        result["weights"], result["places"] = turned[:2], turned[2:]
        last[:] = turned[:1]

    def do_second(c):
        chunk = CHUNKS[c]
        grads = second(
            owns[c], others[c], result["factors"], result["weights"], chunk, cap, 6 in chunk, last
        )
        last[:] = [grads[0]]
        if 6 in chunk:
            result["back"] = swap(grads[0], "expert", 6)
            returned[6] = (result["back"], 0)
        elif 0 in chunk:
            returned[0], result["near"] = (grads[0], 0), grads[1]
        else:
            returned.update({k: (swap(grad, "expert", k), 0) for k, grad in zip(chunk, grads)})

    def do_cross(_):
        both = pair([(result["near"], 0), (result["back"], cap)], cap, last)
        last[:] = [both]
        got = swap(both, "expert", 1)
        returned.update({1: (got, 0), 7: (got, cap)})

    def do_down(_):
        every = [blocks[k] for k in range(groups)]
        result["down"], flag = down(every, result["hidden"], features, last)
        last[:] = [flag]

    def do_gather(part):
        came = [returned[k] for k in PARTS[part]]
        sooner[:] = [gather(result["places"][part], came, cap, sooner, last)]
        last[:] = sooner

    steps = {
        "first": do_first,
        "add": do_add,
        "release": do_release,
        "diagonal": do_diagonal,
        "cross": do_cross,
        "prep": do_prep,
        "turn": do_turn,
        "second": do_second,
        "down": do_down,
        "gather": do_gather,
    }
    for step, c in ORDER:
        steps[step](c)
    came = [returned[k] for k in PARTS[-1]]
    grad_input = finish(result["places"][-1], came, cap, sooner[0], last)
    return (grad_input, result["down"][None])


def far_device(dy_values, dy_scales, expert_ids, saved_pre, w_gate, w_up, w_down):
    groups, width = lax.axis_size("expert"), w_down.shape[2]
    slots = saved_pre.shape[0]
    cap = slots // groups
    route = expert_ids[:, 0]
    rows, count = route.shape[0], dy_scales.shape[1]
    onehot = (route[:, None] == jnp.arange(groups, dtype=jnp.int32)[None, :]).astype(BF16)
    earlier = jnp.dot(jnp.tri(rows, k=-1, dtype=BF16), onehot, preferred_element_type=F32)
    rank = jnp.sum(earlier * onehot.astype(F32), axis=1).astype(jnp.int32)
    place = route * cap + rank
    chosen = (place[:, None] == jnp.arange(slots, dtype=jnp.int32)[None, :]).astype(BF16)
    scaled = dy_values.astype(F32).reshape(rows, count, -1) * dy_scales.astype(F32)[:, :, None]
    scaled = scaled.reshape(dy_values.shape).astype(BF16)
    packed = lax.dot_general(chosen, scaled, BY_ROWS, preferred_element_type=F32).astype(BF16)
    received = lax.all_to_all(packed, "expert", split_axis=0, concat_axis=0, tiled=True)
    gate, up, sigmoid = swish_parts(saved_pre, width)
    hidden = (gate * sigmoid * up).astype(BF16)
    partial = jnp.dot(received, w_down[0], preferred_element_type=F32)
    grad = lax.psum(partial, "dp")
    d_gate = (grad * up * sigmoid * (1.0 + gate * (1.0 - sigmoid))).astype(BF16)
    d_up = (grad * (gate * sigmoid)).astype(BF16)
    result = lax.dot_general(d_gate, w_gate[0], TRANSPOSED, preferred_element_type=F32)
    result += lax.dot_general(d_up, w_up[0], TRANSPOSED, preferred_element_type=F32)
    returned = lax.all_to_all(
        result.astype(BF16), "expert", split_axis=0, concat_axis=0, tiled=True
    )
    grad_input = jnp.dot(chosen, returned, preferred_element_type=F32).astype(BF16)
    grad_down = lax.dot_general(received, hidden, BY_ROWS, preferred_element_type=F32)
    return (grad_input, grad_down[None])


def solution(mesh):
    near = mesh.shape["expert"] == 8 and mesh.shape["dp"] == 4
    return jax.shard_map(
        near_device if near else far_device,
        mesh=mesh,
        in_specs=(
            P("expert", "dp"),
            P("expert", "dp"),
            P("expert", None),
            P("expert", None),
            P("expert", "dp", None),
            P("expert", "dp", None),
            P("expert", "dp", None),
        ),
        out_specs=(P("expert", "dp"), P("expert", "dp", None)),
        check_vma=False,
    )
```

```python
import functools

import jax
import jax.numpy as jnp
from jax import lax
from jax.experimental import pallas as pl
from jax.experimental.pallas import tpu as pltpu
from jax.sharding import PartitionSpec as P

CHUNKS = ((0, 1), (6, 7), (2, 4), (3, 5))
CROSSING, STRAIGHT = (1, 7, 3, 5), (6, 2, 4, 0)
PARTS = (CHUNKS[2], CHUNKS[3], CHUNKS[0] + CHUNKS[1])
ORDER = (
    ("first", 0), ("bundle", 0), ("add", 0), ("prep", 0), ("turn", 0), ("first", 1),
    ("first", 2), ("add", 0), ("add", 1), ("first", 3), ("add", 2), ("add", 1), ("add", 3),
    ("release", 0), ("add", 2), ("second", 1), ("add", 3), ("second", 2), ("second", 3),
    ("second", 0), ("cross", 0), ("down", 0), ("gather", 0), ("gather", 1),
)
HELD = (0,)
COST = {
    "place": 10**10, "pack": 10**10, "rest": 1, "first": 1, "prep": 1, "turn": 1,
    "add": 10**9, "bundle": 1, "second": 10**10, "down": 10**10, "gather": 5 * 10**9, "finish": 1,
}
MIB = 1 << 20
BF16, F32 = jnp.bfloat16, jnp.float32
TRANSPOSED = (((1,), (1,)), ((), ()))
BY_ROWS = (((0,), (0,)), ((), ()))


VMEM, HBM, ANY = (
    pl.BlockSpec(memory_space=space) for space in (pltpu.VMEM, pltpu.HBM, pl.ANY)
)


def call(body, name, operands, specs, outs, out_specs, vmem=16, scratch=(), after=()):
    count, waits = len(operands), len(after)

    def run(*refs):
        body(*refs[:count], *refs[count + waits :])

    return pl.pallas_call(
        run,
        name=name,
        out_shape=outs,
        in_specs=list(specs) + [ANY] * waits,
        out_specs=out_specs,
        scratch_shapes=scratch,
        compiler_params=pltpu.CompilerParams(vmem_limit_bytes=vmem * MIB),
        cost_estimate=pl.CostEstimate(flops=COST[name], bytes_accessed=0, transcendentals=0),
    )(*operands, *after)


def in_hbm(array):
    return pltpu.with_memory_space_constraint(array, pltpu.HBM)


def swish_parts(pre, width):
    gate, up = pre[:, :width].astype(F32), pre[:, width:].astype(F32)
    sigmoid = jax.nn.sigmoid(gate)
    return gate, up, sigmoid


def tiles(size):
    step = 256 if size % 256 == 0 else size
    return [slice(i, i + step) for i in range(0, size, step)]


def arrays_of(blocks):
    found = []
    for array, _ in blocks:
        if not any(array is other for other in found):
            found.append(array)
    return found


def spots_of(blocks, arrays):
    return [(next(i for i, x in enumerate(arrays) if x is array), row) for array, row in blocks]


def rows_at(refs, spots, cap):
    return jnp.concatenate([refs[i][row : row + cap] for i, row in spots], axis=0)


def place_body(groups, cap, ids, place, ids_in, sems):
    bring = pltpu.make_async_copy(ids, ids_in, sems.at[0])
    bring.start()
    rows, slots, lines = ids.shape[1], groups * cap, max(8, groups)
    line = lax.broadcasted_iota(jnp.int32, (lines, rows), 0)
    sooner = lax.broadcasted_iota(jnp.int32, (rows, rows), 0)
    later = lax.broadcasted_iota(jnp.int32, (rows, rows), 1)
    before = jnp.where(sooner < later, 1.0, 0.0).astype(BF16)
    bring.wait()
    route = ids_in[...]
    onehot = jnp.where(line == route, 1.0, 0.0)
    earlier = jnp.dot(onehot.astype(BF16), before, preferred_element_type=F32)
    rank = jnp.sum(earlier * onehot, axis=0, keepdims=True).astype(jnp.int32)
    position = (route ^ lax.axis_index("expert")) * cap + rank
    slot = lax.broadcasted_iota(jnp.int32, (slots, rows), 0)
    place[...] = jnp.where(slot == position, 1.0, 0.0).astype(BF16)


def find_place(ids, groups, cap):
    rows = ids.shape[0]
    return call(
        functools.partial(place_body, groups, cap),
        "place",
        (in_hbm(ids.T),),
        (HBM,),
        [jax.ShapeDtypeStruct((groups * cap, rows), BF16)],
        [VMEM],
        16,
        [pltpu.VMEM((1, rows), jnp.int32), pltpu.SemaphoreType.DMA((1,))],
    )[0]


def put_blocks(place, rows, outs, groups, cap):
    chosen = rows_at([place], [(0, k * cap) for group in groups for k in group], cap)
    for part in tiles(rows.shape[1]):
        packed = jnp.dot(chosen, rows[:, part], preferred_element_type=F32).astype(BF16)
        start = 0
        for group, out in zip(groups, outs):
            out[:, part] = packed[start : start + len(group) * cap]
            start += len(group) * cap


def pack_body(groups, cap, place, scales, values, scaled, *outs):
    features, count = values.shape[1], scales.shape[0]
    owner = lax.broadcasted_iota(jnp.int32, (count, features), 1) // (features // count)
    spread = jnp.where(owner == lax.broadcasted_iota(jnp.int32, (count, features), 0), 1.0, 0.0)
    spread = spread.astype(BF16)
    for part in tiles(features):
        factor = lax.dot_general(
            scales[...], spread[:, part], BY_ROWS, preferred_element_type=F32
        )
        scaled[:, part] = (values[:, part].astype(F32) * factor).astype(BF16)
    put_blocks(place, scaled, outs, groups, cap)


def rest_body(groups, cap, place, scaled, *outs):
    put_blocks(place, scaled, outs, groups, cap)


def pack(place, values, scales, groups, cap):
    rows, features = values.shape
    return call(
        functools.partial(pack_body, groups, cap),
        "pack",
        (place, scales.T, values),
        [VMEM] * 3,
        [jax.ShapeDtypeStruct((rows, features), BF16)]
        + [jax.ShapeDtypeStruct((len(group) * cap, features), BF16) for group in groups],
        [VMEM] * (1 + len(groups)),
    )


def pack_rest(place, scaled, groups, cap, after):
    features = scaled.shape[1]
    return call(
        functools.partial(rest_body, groups, cap),
        "rest",
        (place, scaled),
        [VMEM] * 2,
        [jax.ShapeDtypeStruct((len(group) * cap, features), BF16) for group in groups],
        [VMEM] * len(groups),
        after=after,
    )


def bundle_body(count, groups, cap, *refs):
    for spots, out in zip(groups, refs[count:]):
        out[...] = rows_at(refs[:count], spots, cap)


def bundle(groups, cap, after):
    arrays = arrays_of([block for blocks in groups for block in blocks])
    width = arrays[0].shape[1]
    return call(
        functools.partial(
            bundle_body, len(arrays), [spots_of(blocks, arrays) for blocks in groups], cap
        ),
        "bundle",
        arrays,
        [VMEM] * len(arrays),
        [jax.ShapeDtypeStruct((len(blocks) * cap, width), BF16) for blocks in groups],
        [VMEM] * len(groups),
        after=after,
    )


def first_body(count, spots, cap, weight, *refs):
    arrays, send, keep, both = refs[:count], *refs[count:]
    rows = rows_at(arrays, spots, cap)
    width = weight.shape[1]
    for part in tiles(width):
        both[:, part] = jnp.dot(rows, weight[:, part], preferred_element_type=F32)
    halves = [slice(0, width // 2), slice(width // 2, width)]
    for odd, (theirs, mine) in enumerate((reversed(halves), halves)):

        @pl.when(lax.axis_index("dp") % 2 == odd)
        def _():
            send[...] = both[:, theirs].astype(BF16)
            keep[...] = both[:, mine]


def first(blocks, weight, cap, after):
    arrays = arrays_of(blocks)
    features, width = weight.shape
    size = len(blocks) * cap
    return call(
        functools.partial(first_body, len(arrays), spots_of(blocks, arrays), cap),
        "first",
        (weight, *arrays),
        [VMEM] * (1 + len(arrays)),
        [jax.ShapeDtypeStruct((size, width // 2), dtype) for dtype in (BF16, F32)],
        [VMEM] * 2,
        16,
        [pltpu.VMEM((size, width), F32)],
        after=after,
    )


def add_body(rows, *refs):
    total = 0.0
    for ref, row in zip(refs, rows):
        total += ref[row : row + refs[-1].shape[0]].astype(F32)
    refs[-1][...] = total.astype(BF16)


def add(terms, size, after):
    return call(
        functools.partial(add_body, [row for _, row in terms]),
        "add",
        [array for array, _ in terms],
        [VMEM] * len(terms),
        [jax.ShapeDtypeStruct((size, terms[0][0].shape[1]), BF16)],
        [VMEM],
        8,
        after=after,
    )[0]


def prep_body(saved, gate_factor, up_factor, hidden):
    slots, width = hidden.shape
    step = 32 if slots % 32 == 0 else slots

    def some(i, carry):
        at = pl.ds(pl.multiple_of(i * step, step), step)
        gate, up, sigmoid = swish_parts(saved[at, :], width)
        silu = gate * sigmoid
        gate_factor[at, :] = up * sigmoid * (1.0 + gate * (1.0 - sigmoid))
        up_factor[at, :] = silu
        hidden[at, :] = (silu * up).astype(BF16)
        return carry

    lax.fori_loop(0, slots // step, some, 0)


def prep(saved_pre, after):
    slots, width = saved_pre.shape[0], saved_pre.shape[1] // 2
    return call(
        prep_body,
        "prep",
        (saved_pre,),
        [VMEM],
        [jax.ShapeDtypeStruct((slots, width), dtype) for dtype in (F32, F32, BF16)],
        [VMEM] * 3,
        16,
        after=after,
    )


def turn_body(count, cap, groups, place, *refs):
    weights, turned, places = refs[:count], refs[count : 2 * count], refs[2 * count :]
    for weight, out in zip(weights, turned):
        for part in tiles(weight.shape[0]):
            out[:, part] = weight[part, :].T
    for group, out in zip(groups, places):
        out[...] = rows_at([place], [(0, k * cap) for k in group], cap).T


def turn(weights, place, groups, cap, after):
    count, rows = len(weights), place.shape[1]
    return call(
        functools.partial(turn_body, count, cap, groups),
        "turn",
        (place, *weights),
        [VMEM] * (1 + count),
        [jax.ShapeDtypeStruct(x.shape[::-1], x.dtype) for x in weights]
        + [jax.ShapeDtypeStruct((rows, len(group) * cap), BF16) for group in groups],
        [VMEM] * (count + len(groups)),
        16,
        after=after,
    )


def slots_of(ref, k, cap):
    start = pl.multiple_of((lax.axis_index("expert") ^ k) * cap, cap)
    return ref[pl.ds(start, cap), :]


def second_body(chunk, cap, row, own, other, gate_factor, up_factor, w_gate, w_up, *refs):
    outs, grads = refs[:-1], refs[-1]
    width, features = w_gate.shape
    halves = [slice(0, width // 2), slice(width // 2, width)]
    for odd, (theirs, mine) in enumerate((reversed(halves), halves)):

        @pl.when(lax.axis_index("dp") % 2 == odd)
        def _():
            grads[:, mine] = own[...]
            grads[:, theirs] = other[row : row + own.shape[0]]

    grad = grads[...].astype(F32)
    d_gate, d_up = (
        (grad * jnp.concatenate([slots_of(factor, k, cap) for k in chunk], axis=0))
        .astype(BF16)
        for factor in (gate_factor, up_factor)
    )
    for part in tiles(features):
        result = jnp.dot(d_gate, w_gate[:, part], preferred_element_type=F32)
        result += jnp.dot(d_up, w_up[:, part], preferred_element_type=F32)
        result = result.astype(BF16)
        size = result.shape[0] // len(outs)
        for i, out in enumerate(outs):
            out[:, part] = result[i * size : (i + 1) * size]


def second(own, other, factors, weights, chunk, cap, together, after):
    width, features = weights[0].shape
    count = 1 if together else len(chunk)
    size = len(chunk) // count * cap
    return call(
        functools.partial(second_body, chunk, cap, other[1]),
        "second",
        (own, other[0], *factors, *weights),
        [VMEM] * 6,
        [jax.ShapeDtypeStruct((size, features), BF16)] * count,
        [VMEM] * count,
        24,
        [pltpu.VMEM((len(chunk) * cap, width), BF16)],
        after=after,
    )


def down_body(count, spots, hidden, *refs):
    arrays, out, flag, sums, sems = refs[:count], *refs[count:]
    flag[...] = jnp.zeros_like(flag)
    cap = hidden.shape[0] // len(spots)
    features, width = out.shape
    mine = jnp.concatenate([slots_of(hidden, k, cap) for k in range(len(spots))], axis=0)
    tile = sums.shape[1]
    copies = []
    for i in range(features // tile):
        part = [arrays[a][row : row + cap, i * tile : (i + 1) * tile] for a, row in spots]
        part = jnp.concatenate(part, axis=0)
        sums[i] = lax.dot_general(part, mine, BY_ROWS, preferred_element_type=F32)
        copies.append(
            pltpu.make_async_copy(sums.at[i], out.at[pl.ds(i * tile, tile)], sems.at[i])
        )
        copies[-1].start()
    for copy in copies:
        copy.wait()


def down(blocks, hidden, features, after):
    arrays = arrays_of(blocks)
    slots, width = hidden.shape
    tile = min(features, 256)
    steps = features // tile
    return call(
        functools.partial(down_body, len(arrays), spots_of(blocks, arrays)),
        "down",
        (hidden, *arrays),
        [VMEM] * (1 + len(arrays)),
        [jax.ShapeDtypeStruct((features, width), F32), jax.ShapeDtypeStruct((8, 128), F32)],
        [HBM, VMEM],
        24,
        [pltpu.VMEM((steps, tile, width), F32), pltpu.SemaphoreType.DMA((steps,))],
        after=after,
    )


def rows_of(place, arrays, spots, cap, part):
    returned = [arrays[i][row : row + cap, part] for i, row in spots]
    returned = jnp.concatenate(returned, axis=0)
    return jnp.dot(place[...], returned, preferred_element_type=F32).astype(BF16)


def gather_body(count, spots, cap, place, *refs):
    arrays, sooner, out = refs[:count], refs[count:-1], refs[-1]
    for part in tiles(out.shape[1]):
        rows = rows_of(place, arrays, spots, cap, part)
        for others in sooner:
            rows += others[:, part]
        out[:, part] = rows


def gather(place, blocks, cap, sooner, after):
    arrays = arrays_of(blocks)
    rows, features = place.shape[0], arrays[0].shape[1]
    return call(
        functools.partial(gather_body, len(arrays), spots_of(blocks, arrays), cap),
        "gather",
        (place, *arrays, *sooner),
        [VMEM] * (1 + len(arrays) + len(sooner)),
        [jax.ShapeDtypeStruct((rows, features), BF16)],
        [VMEM],
        16,
        after=after,
    )[0]


def finish_body(count, spots, cap, place, sooner, *refs):
    arrays, out, whole, sems = refs[:count], *refs[count:]
    copies = []
    for i, part in enumerate(tiles(out.shape[1])):
        whole[:, part] = rows_of(place, arrays, spots, cap, part) + sooner[:, part]
        copies.append(pltpu.make_async_copy(whole.at[:, part], out.at[:, part], sems.at[i]))
        copies[-1].start()
    for copy in copies:
        copy.wait()


def finish(place, blocks, cap, sooner, after):
    arrays, (rows, features) = arrays_of(blocks), sooner.shape
    return call(
        functools.partial(finish_body, len(arrays), spots_of(blocks, arrays), cap),
        "finish",
        (place, sooner, *arrays),
        [VMEM] * (2 + len(arrays)),
        [jax.ShapeDtypeStruct((rows, features), BF16)],
        [HBM],
        16,
        [
            pltpu.VMEM((rows, features), BF16),
            pltpu.SemaphoreType.DMA((len(tiles(features)),)),
        ],
        after=after,
    )[0]


def swap(block, axis, k):
    size = lax.axis_size(axis)
    return lax.ppermute(block, axis, [(i, i ^ k) for i in range(size)])


def near_device(dy_values, dy_scales, expert_ids, saved_pre, w_gate, w_up, w_down):
    groups = lax.axis_size("expert")
    cap = saved_pre.shape[0] // groups
    features = dy_values.shape[1]
    terms, owns, others, returned, result = {}, {}, {}, {}, {}

    place = find_place(expert_ids, groups, cap)
    last, sooner = [place], []
    scaled, crossing = pack(place, dy_values, dy_scales, (CROSSING,), cap)
    side = swap(crossing, "expert", 1)
    (ahead,) = pack_rest(place, scaled, (STRAIGHT,), cap, [crossing])
    last[:] = [ahead]
    blocks = {1: (side, 0), 0: (ahead, STRAIGHT.index(0) * cap)}

    def do_bundle(_):
        chips = [k for k in STRAIGHT if k]
        groups = [
            ((ahead, STRAIGHT.index(k) * cap), (side, CROSSING.index(k + 1) * cap)) for k in chips
        ]
        bundles = bundle(groups, cap, last)
        last[:] = bundles[:1]
        for k, both in zip(chips, bundles):
            got = swap(both, "expert", k)
            blocks.update({k: (got, 0), k + 1: (got, cap)})

    def do_first(c):
        send, keep = first([blocks[k] for k in CHUNKS[c]], w_down[0], cap, last)
        last[:] = [send]
        terms[c] = [(keep, 0), (swap(send, "dp", 1), 0)]

    def do_add(c):
        size = len(CHUNKS[c]) * cap
        part = add(terms[c], size, last)
        last[:] = [part]
        if len(terms[c]) == 2:
            terms[c].append((swap(part, "dp", 2), 0))
        else:
            owns[c] = part
            if c not in HELD:
                others[c] = (swap(part, "dp", 1), 0)

    def do_release(c):
        (total,) = bundle([[(owns[c], 0)]], len(CHUNKS[c]) * cap, last)
        last[:] = [total]
        others[c] = (swap(total, "dp", 1), 0)

    def do_prep(_):
        *result["factors"], result["hidden"] = prep(saved_pre, last)
        last[:] = [result["hidden"]]

    def do_turn(_):
        turned = turn((w_gate[0], w_up[0]), place, PARTS, cap, last)
        result["weights"], result["places"] = turned[:2], turned[2:]
        last[:] = turned[:1]

    def do_second(c):
        chunk = CHUNKS[c]
        grads = second(
            owns[c], others[c], result["factors"], result["weights"], chunk, cap, 6 in chunk, last
        )
        last[:] = [grads[0]]
        if 6 in chunk:
            result["back"] = swap(grads[0], "expert", 6)
            returned[6] = (result["back"], 0)
        elif 0 in chunk:
            returned[0], result["near"] = (grads[0], 0), grads[1]
        else:
            returned.update({k: (swap(grad, "expert", k), 0) for k, grad in zip(chunk, grads)})

    def do_cross(_):
        (both,) = bundle([[(result["near"], 0), (result["back"], cap)]], cap, last)
        last[:] = [both]
        got = swap(both, "expert", 1)
        returned.update({1: (got, 0), 7: (got, cap)})

    def do_down(_):
        every = [blocks[k] for k in range(groups)]
        result["down"], flag = down(every, result["hidden"], features, last)
        last[:] = [flag]

    def do_gather(part):
        came = [returned[k] for k in PARTS[part]]
        sooner[:] = [gather(result["places"][part], came, cap, sooner, last)]
        last[:] = sooner

    steps = {
        "first": do_first,
        "add": do_add,
        "release": do_release,
        "bundle": do_bundle,
        "cross": do_cross,
        "prep": do_prep,
        "turn": do_turn,
        "second": do_second,
        "down": do_down,
        "gather": do_gather,
    }
    for step, c in ORDER:
        steps[step](c)
    came = [returned[k] for k in PARTS[-1]]
    grad_input = finish(result["places"][-1], came, cap, sooner[0], last)
    return (grad_input, result["down"][None])


def far_device(dy_values, dy_scales, expert_ids, saved_pre, w_gate, w_up, w_down):
    groups, width = lax.axis_size("expert"), w_down.shape[2]
    slots = saved_pre.shape[0]
    cap = slots // groups
    route = expert_ids[:, 0]
    rows, count = route.shape[0], dy_scales.shape[1]
    onehot = (route[:, None] == jnp.arange(groups, dtype=jnp.int32)[None, :]).astype(BF16)
    earlier = jnp.dot(jnp.tri(rows, k=-1, dtype=BF16), onehot, preferred_element_type=F32)
    rank = jnp.sum(earlier * onehot.astype(F32), axis=1).astype(jnp.int32)
    place = route * cap + rank
    chosen = (place[:, None] == jnp.arange(slots, dtype=jnp.int32)[None, :]).astype(BF16)
    scaled = dy_values.astype(F32).reshape(rows, count, -1) * dy_scales.astype(F32)[:, :, None]
    scaled = scaled.reshape(dy_values.shape).astype(BF16)
    packed = lax.dot_general(chosen, scaled, BY_ROWS, preferred_element_type=F32).astype(BF16)
    received = lax.all_to_all(packed, "expert", split_axis=0, concat_axis=0, tiled=True)
    gate, up, sigmoid = swish_parts(saved_pre, width)
    hidden = (gate * sigmoid * up).astype(BF16)
    partial = jnp.dot(received, w_down[0], preferred_element_type=F32)
    grad = lax.psum(partial, "dp")
    d_gate = (grad * up * sigmoid * (1.0 + gate * (1.0 - sigmoid))).astype(BF16)
    d_up = (grad * (gate * sigmoid)).astype(BF16)
    result = lax.dot_general(d_gate, w_gate[0], TRANSPOSED, preferred_element_type=F32)
    result += lax.dot_general(d_up, w_up[0], TRANSPOSED, preferred_element_type=F32)
    returned = lax.all_to_all(
        result.astype(BF16), "expert", split_axis=0, concat_axis=0, tiled=True
    )
    grad_input = jnp.dot(chosen, returned, preferred_element_type=F32).astype(BF16)
    grad_down = lax.dot_general(received, hidden, BY_ROWS, preferred_element_type=F32)
    return (grad_input, grad_down[None])


def solution(mesh):
    near = mesh.shape["expert"] == 8 and mesh.shape["dp"] == 4
    return jax.shard_map(
        near_device if near else far_device,
        mesh=mesh,
        in_specs=(
            P("expert", "dp"),
            P("expert", "dp"),
            P("expert", None),
            P("expert", None),
            P("expert", "dp", None),
            P("expert", "dp", None),
            P("expert", "dp", None),
        ),
        out_specs=(P("expert", "dp"), P("expert", "dp", None)),
        check_vma=False,
    )
```

```python
import functools

import jax
import jax.numpy as jnp
from jax import lax
from jax.experimental import pallas as pl
from jax.experimental.pallas import tpu as pltpu
from jax.sharding import PartitionSpec as P

CHUNKS = ((0, 1), (6, 7), (2, 4), (3, 5))
LATER = (2, 4, 3, 5, 0)
PARTS = (CHUNKS[2], CHUNKS[0] + CHUNKS[1], CHUNKS[3])
ORDER = (
    ("first", 0), ("diagonal", 0), ("add", 0), ("prep", 0), ("turn", 0), ("first", 1),
    ("first", 2), ("add", 0), ("add", 1), ("first", 3), ("add", 2), ("add", 1), ("add", 3),
    ("down", 0), ("add", 2), ("release", 0), ("add", 3), ("second", 1), ("second", 2),
    ("second", 3), ("second", 0), ("cross", 0), ("gather", 0), ("gather", 1),
)
HELD = (0,)
COST = {
    "place": 10**10, "pack": 10**10, "rest": 1, "first": 1, "prep": 1, "turn": 1,
    "add": 10**9, "release": 1, "pair": 1, "second": 10**10, "down": 1, "gather": 5 * 10**9, "finish": 1,
}
MIB = 1 << 20
BF16, F32 = jnp.bfloat16, jnp.float32
TRANSPOSED = (((1,), (1,)), ((), ()))
BY_ROWS = (((0,), (0,)), ((), ()))


VMEM, HBM, ANY = (
    pl.BlockSpec(memory_space=space) for space in (pltpu.VMEM, pltpu.HBM, pl.ANY)
)


def call(body, name, operands, specs, outs, out_specs, vmem=16, scratch=(), after=()):
    count, waits = len(operands), len(after)

    def run(*refs):
        body(*refs[:count], *refs[count + waits :])

    return pl.pallas_call(
        run,
        name=name,
        out_shape=outs,
        in_specs=list(specs) + [ANY] * waits,
        out_specs=out_specs,
        scratch_shapes=scratch,
        compiler_params=pltpu.CompilerParams(vmem_limit_bytes=vmem * MIB),
        cost_estimate=pl.CostEstimate(flops=COST[name], bytes_accessed=0, transcendentals=0),
    )(*operands, *after)


def in_hbm(array):
    return pltpu.with_memory_space_constraint(array, pltpu.HBM)


def swish_parts(pre, width):
    gate, up = pre[:, :width].astype(F32), pre[:, width:].astype(F32)
    sigmoid = jax.nn.sigmoid(gate)
    return gate, up, sigmoid


def tiles(size):
    step = 256 if size % 256 == 0 else size
    return [slice(i, i + step) for i in range(0, size, step)]


def arrays_of(blocks):
    found = []
    for array, _ in blocks:
        if not any(array is other for other in found):
            found.append(array)
    return found


def spots_of(blocks, arrays):
    return [(next(i for i, x in enumerate(arrays) if x is array), row) for array, row in blocks]


def rows_at(refs, spots, cap):
    return jnp.concatenate([refs[i][row : row + cap] for i, row in spots], axis=0)


def place_body(groups, cap, ids, place, ids_in, sems):
    bring = pltpu.make_async_copy(ids, ids_in, sems.at[0])
    bring.start()
    rows, slots, lines = ids.shape[1], groups * cap, max(8, groups)
    line = lax.broadcasted_iota(jnp.int32, (lines, rows), 0)
    sooner = lax.broadcasted_iota(jnp.int32, (rows, rows), 0)
    later = lax.broadcasted_iota(jnp.int32, (rows, rows), 1)
    before = jnp.where(sooner < later, 1.0, 0.0).astype(BF16)
    bring.wait()
    route = ids_in[...]
    onehot = jnp.where(line == route, 1.0, 0.0)
    earlier = jnp.dot(onehot.astype(BF16), before, preferred_element_type=F32)
    rank = jnp.sum(earlier * onehot, axis=0, keepdims=True).astype(jnp.int32)
    position = (route ^ lax.axis_index("expert")) * cap + rank
    slot = lax.broadcasted_iota(jnp.int32, (slots, rows), 0)
    place[...] = jnp.where(slot == position, 1.0, 0.0).astype(BF16)


def find_place(ids, groups, cap):
    rows = ids.shape[0]
    return call(
        functools.partial(place_body, groups, cap),
        "place",
        (in_hbm(ids.T),),
        (HBM,),
        [jax.ShapeDtypeStruct((groups * cap, rows), BF16)],
        [VMEM],
        16,
        [pltpu.VMEM((1, rows), jnp.int32), pltpu.SemaphoreType.DMA((1,))],
    )[0]


def put_blocks(place, rows, outs, groups, cap):
    chosen = rows_at([place], [(0, k * cap) for group in groups for k in group], cap)
    for part in tiles(rows.shape[1]):
        packed = jnp.dot(chosen, rows[:, part], preferred_element_type=F32).astype(BF16)
        start = 0
        for group, out in zip(groups, outs):
            out[:, part] = packed[start : start + len(group) * cap]
            start += len(group) * cap


def pack_body(groups, cap, place, scales, values, scaled, *outs):
    features, count = values.shape[1], scales.shape[0]
    owner = lax.broadcasted_iota(jnp.int32, (count, features), 1) // (features // count)
    spread = jnp.where(owner == lax.broadcasted_iota(jnp.int32, (count, features), 0), 1.0, 0.0)
    spread = spread.astype(BF16)
    for part in tiles(features):
        factor = lax.dot_general(
            scales[...], spread[:, part], BY_ROWS, preferred_element_type=F32
        )
        scaled[:, part] = (values[:, part].astype(F32) * factor).astype(BF16)
    put_blocks(place, scaled, outs, groups, cap)


def rest_body(groups, cap, place, scaled, *outs):
    put_blocks(place, scaled, outs, groups, cap)


def pack(place, values, scales, groups, cap):
    rows, features = values.shape
    return call(
        functools.partial(pack_body, groups, cap),
        "pack",
        (place, scales.T, values),
        [VMEM] * 3,
        [jax.ShapeDtypeStruct((rows, features), BF16)]
        + [jax.ShapeDtypeStruct((len(group) * cap, features), BF16) for group in groups],
        [VMEM] * (1 + len(groups)),
    )


def pack_rest(place, scaled, groups, cap, after):
    features = scaled.shape[1]
    return call(
        functools.partial(rest_body, groups, cap),
        "rest",
        (place, scaled),
        [VMEM] * 2,
        [jax.ShapeDtypeStruct((len(group) * cap, features), BF16) for group in groups],
        [VMEM] * len(groups),
        after=after,
    )


def pair_body(count, spots, cap, *refs):
    refs[count][...] = rows_at(refs[:count], spots, cap)


def pair(blocks, cap, after):
    arrays = arrays_of(blocks)
    shape = jax.ShapeDtypeStruct((len(blocks) * cap, arrays[0].shape[1]), BF16)
    return call(
        functools.partial(pair_body, len(arrays), spots_of(blocks, arrays), cap),
        "pair",
        arrays,
        [VMEM] * len(arrays),
        [shape],
        [VMEM],
        after=after,
    )[0]


def first_body(count, spots, cap, weight, *refs):
    arrays, send, keep, both = refs[:count], *refs[count:]
    rows = rows_at(arrays, spots, cap)
    width = weight.shape[1]
    for part in tiles(width):
        both[:, part] = jnp.dot(rows, weight[:, part], preferred_element_type=F32)
    halves = [slice(0, width // 2), slice(width // 2, width)]
    for odd, (theirs, mine) in enumerate((reversed(halves), halves)):

        @pl.when(lax.axis_index("dp") % 2 == odd)
        def _():
            send[...] = both[:, theirs].astype(BF16)
            keep[...] = both[:, mine]


def first(blocks, weight, cap, after):
    arrays = arrays_of(blocks)
    features, width = weight.shape
    size = len(blocks) * cap
    return call(
        functools.partial(first_body, len(arrays), spots_of(blocks, arrays), cap),
        "first",
        (weight, *arrays),
        [VMEM] * (1 + len(arrays)),
        [jax.ShapeDtypeStruct((size, width // 2), dtype) for dtype in (BF16, F32)],
        [VMEM] * 2,
        16,
        [pltpu.VMEM((size, width), F32)],
        after=after,
    )


def add_body(count, keep, *refs):
    total = keep[...]
    for got in refs[:count]:
        total = total + got[...].astype(F32)
    refs[count][...] = total.astype(BF16)


def add(keep, gots, after):
    return call(
        functools.partial(add_body, len(gots)),
        "add",
        (keep, *gots),
        [VMEM] * (1 + len(gots)),
        [jax.ShapeDtypeStruct(keep.shape, BF16)],
        [VMEM],
        16,
        after=after,
    )[0]


def release_body(total, out):
    out[...] = total[...]


def release(total, after):
    shape = jax.ShapeDtypeStruct(total.shape, total.dtype)
    return call(release_body, "release", (total,), [VMEM], [shape], [VMEM], after=after)[0]


def prep_body(saved, gate_factor, up_factor, hidden):
    slots, width = hidden.shape
    step = 32 if slots % 32 == 0 else slots

    def some(i, carry):
        at = pl.ds(pl.multiple_of(i * step, step), step)
        gate, up, sigmoid = swish_parts(saved[at, :], width)
        silu = gate * sigmoid
        gate_factor[at, :] = up * sigmoid * (1.0 + gate * (1.0 - sigmoid))
        up_factor[at, :] = silu
        hidden[at, :] = (silu * up).astype(BF16)
        return carry

    lax.fori_loop(0, slots // step, some, 0)


def prep(saved_pre, after):
    slots, width = saved_pre.shape[0], saved_pre.shape[1] // 2
    return call(
        prep_body,
        "prep",
        (saved_pre,),
        [VMEM],
        [jax.ShapeDtypeStruct((slots, width), dtype) for dtype in (F32, F32, BF16)],
        [VMEM] * 3,
        16,
        after=after,
    )


def turn_body(count, cap, groups, place, *refs):
    weights, turned, places = refs[:count], refs[count : 2 * count], refs[2 * count :]
    for weight, out in zip(weights, turned):
        for part in tiles(weight.shape[0]):
            out[:, part] = weight[part, :].T
    for group, out in zip(groups, places):
        out[...] = rows_at([place], [(0, k * cap) for k in group], cap).T


def turn(weights, place, groups, cap, after):
    count, rows = len(weights), place.shape[1]
    return call(
        functools.partial(turn_body, count, cap, groups),
        "turn",
        (place, *weights),
        [VMEM] * (1 + count),
        [jax.ShapeDtypeStruct(x.shape[::-1], x.dtype) for x in weights]
        + [jax.ShapeDtypeStruct((rows, len(group) * cap), BF16) for group in groups],
        [VMEM] * (count + len(groups)),
        16,
        after=after,
    )


def slots_of(ref, k, cap):
    start = pl.multiple_of((lax.axis_index("expert") ^ k) * cap, cap)
    return ref[pl.ds(start, cap), :]


def second_body(chunk, cap, own, other, gate_factor, up_factor, w_gate, w_up, *refs):
    outs, grads = refs[:-1], refs[-1]
    width, features = w_gate.shape
    halves = [slice(0, width // 2), slice(width // 2, width)]
    for odd, (theirs, mine) in enumerate((reversed(halves), halves)):

        @pl.when(lax.axis_index("dp") % 2 == odd)
        def _():
            grads[:, mine] = own[...]
            grads[:, theirs] = other[...]

    grad = grads[...].astype(F32)
    d_gate, d_up = (
        (grad * jnp.concatenate([slots_of(factor, k, cap) for k in chunk], axis=0))
        .astype(BF16)
        for factor in (gate_factor, up_factor)
    )
    for part in tiles(features):
        result = jnp.dot(d_gate, w_gate[:, part], preferred_element_type=F32)
        result += jnp.dot(d_up, w_up[:, part], preferred_element_type=F32)
        result = result.astype(BF16)
        size = result.shape[0] // len(outs)
        for i, out in enumerate(outs):
            out[:, part] = result[i * size : (i + 1) * size]


def second(own, other, factors, weights, chunk, cap, together, after):
    width, features = weights[0].shape
    count = 1 if together else len(chunk)
    size = len(chunk) // count * cap
    return call(
        functools.partial(second_body, chunk, cap),
        "second",
        (own, other, *factors, *weights),
        [VMEM] * 6,
        [jax.ShapeDtypeStruct((size, features), BF16)] * count,
        [VMEM] * count,
        24,
        [pltpu.VMEM((len(chunk) * cap, width), BF16)],
        after=after,
    )


def down_body(count, spots, hidden, *refs):
    arrays, out, flag, sums, sems = refs[:count], *refs[count:]
    flag[...] = jnp.zeros_like(flag)
    cap = hidden.shape[0] // len(spots)
    features, width = out.shape
    mine = jnp.concatenate([slots_of(hidden, k, cap) for k in range(len(spots))], axis=0)
    tile = sums.shape[1]
    copies = []
    for i in range(features // tile):
        part = [arrays[a][row : row + cap, i * tile : (i + 1) * tile] for a, row in spots]
        part = jnp.concatenate(part, axis=0)
        sums[i] = lax.dot_general(part, mine, BY_ROWS, preferred_element_type=F32)
        copies.append(
            pltpu.make_async_copy(sums.at[i], out.at[pl.ds(i * tile, tile)], sems.at[i])
        )
        copies[-1].start()
    for copy in copies:
        copy.wait()


def down(blocks, hidden, features, after):
    arrays = arrays_of(blocks)
    slots, width = hidden.shape
    tile = min(features, 256)
    steps = features // tile
    return call(
        functools.partial(down_body, len(arrays), spots_of(blocks, arrays)),
        "down",
        (hidden, *arrays),
        [VMEM] * (1 + len(arrays)),
        [jax.ShapeDtypeStruct((features, width), F32), jax.ShapeDtypeStruct((8, 128), F32)],
        [HBM, VMEM],
        24,
        [pltpu.VMEM((steps, tile, width), F32), pltpu.SemaphoreType.DMA((steps,))],
        after=after,
    )


def rows_of(place, arrays, spots, cap, part):
    returned = [arrays[i][row : row + cap, part] for i, row in spots]
    returned = jnp.concatenate(returned, axis=0)
    return jnp.dot(place[...], returned, preferred_element_type=F32).astype(BF16)


def gather_body(count, spots, cap, place, *refs):
    arrays, sooner, out = refs[:count], refs[count:-1], refs[-1]
    for part in tiles(out.shape[1]):
        rows = rows_of(place, arrays, spots, cap, part)
        for others in sooner:
            rows += others[:, part]
        out[:, part] = rows


def gather(place, blocks, cap, sooner, after):
    arrays = arrays_of(blocks)
    rows, features = place.shape[0], arrays[0].shape[1]
    return call(
        functools.partial(gather_body, len(arrays), spots_of(blocks, arrays), cap),
        "gather",
        (place, *arrays, *sooner),
        [VMEM] * (1 + len(arrays) + len(sooner)),
        [jax.ShapeDtypeStruct((rows, features), BF16)],
        [VMEM],
        16,
        after=after,
    )[0]


def finish_body(count, spots, cap, place, sooner, *refs):
    arrays, out, whole, sems = refs[:count], *refs[count:]
    copies = []
    for i, part in enumerate(tiles(out.shape[1])):
        whole[:, part] = rows_of(place, arrays, spots, cap, part) + sooner[:, part]
        copies.append(pltpu.make_async_copy(whole.at[:, part], out.at[:, part], sems.at[i]))
        copies[-1].start()
    for copy in copies:
        copy.wait()


def finish(place, blocks, cap, sooner, after):
    arrays, (rows, features) = arrays_of(blocks), sooner.shape
    return call(
        functools.partial(finish_body, len(arrays), spots_of(blocks, arrays), cap),
        "finish",
        (place, sooner, *arrays),
        [VMEM] * (2 + len(arrays)),
        [jax.ShapeDtypeStruct((rows, features), BF16)],
        [HBM],
        16,
        [
            pltpu.VMEM((rows, features), BF16),
            pltpu.SemaphoreType.DMA((len(tiles(features)),)),
        ],
        after=after,
    )[0]


def swap(block, axis, k):
    size = lax.axis_size(axis)
    return lax.ppermute(block, axis, [(i, i ^ k) for i in range(size)])


def near_device(dy_values, dy_scales, expert_ids, saved_pre, w_gate, w_up, w_down):
    groups = lax.axis_size("expert")
    cap = saved_pre.shape[0] // groups
    features = dy_values.shape[1]
    keeps, gots, owns, others, returned, result = {}, {}, {}, {}, {}, {}

    place = find_place(expert_ids, groups, cap)
    last, sooner = [place], []
    scaled, crossing, ahead = pack(place, dy_values, dy_scales, ((1, 7), (6,)), cap)
    side = swap(crossing, "expert", 1)
    rest = pack_rest(place, scaled, [(k,) for k in LATER], cap, [crossing])
    last[:] = rest[-1:]
    blocks = {1: (side, 0)}
    for k, block in zip(LATER, rest):
        blocks[k] = (swap(block, "expert", k) if k else block, 0)

    def do_diagonal(_):
        both = pair([(ahead, 0), (side, cap)], cap, last)
        last[:] = [both]
        got = swap(both, "expert", 6)
        blocks.update({6: (got, 0), 7: (got, cap)})

    def do_first(c):
        send, keeps[c] = first([blocks[k] for k in CHUNKS[c]], w_down[0], cap, last)
        last[:] = [send]
        gots[c] = [swap(send, "dp", 1)]

    def do_add(c):
        part = add(keeps[c], gots[c], last)
        last[:] = [part]
        if len(gots[c]) == 1:
            gots[c].append(swap(part, "dp", 2))
        elif c in HELD:
            owns[c] = part
        else:
            owns[c], others[c] = part, swap(part, "dp", 1)

    def do_release(c):
        owns[c] = release(owns[c], last)
        last[:] = [owns[c]]
        others[c] = swap(owns[c], "dp", 1)

    def do_prep(_):
        *result["factors"], result["hidden"] = prep(saved_pre, last)
        last[:] = [result["hidden"]]

    def do_turn(_):
        turned = turn((w_gate[0], w_up[0]), place, PARTS, cap, last)
        result["weights"], result["places"] = turned[:2], turned[2:]
        last[:] = turned[:1]

    def do_second(c):
        chunk = CHUNKS[c]
        grads = second(
            owns[c], others[c], result["factors"], result["weights"], chunk, cap, 6 in chunk, last
        )
        last[:] = [grads[0]]
        if 6 in chunk:
            result["back"] = swap(grads[0], "expert", 6)
            returned[6] = (result["back"], 0)
        elif 0 in chunk:
            returned[0], result["near"] = (grads[0], 0), grads[1]
        else:
            returned.update({k: (swap(grad, "expert", k), 0) for k, grad in zip(chunk, grads)})

    def do_cross(_):
        both = pair([(result["near"], 0), (result["back"], cap)], cap, last)
        last[:] = [both]
        got = swap(both, "expert", 1)
        returned.update({1: (got, 0), 7: (got, cap)})

    def do_down(_):
        every = [blocks[k] for k in range(groups)]
        result["down"], flag = down(every, result["hidden"], features, last)
        last[:] = [flag]

    def do_gather(part):
        came = [returned[k] for k in PARTS[part]]
        sooner[:] = [gather(result["places"][part], came, cap, sooner, last)]
        last[:] = sooner

    steps = {
        "first": do_first,
        "add": do_add,
        "release": do_release,
        "diagonal": do_diagonal,
        "cross": do_cross,
        "prep": do_prep,
        "turn": do_turn,
        "second": do_second,
        "down": do_down,
        "gather": do_gather,
    }
    for step, c in ORDER:
        steps[step](c)
    came = [returned[k] for k in PARTS[-1]]
    grad_input = finish(result["places"][-1], came, cap, sooner[0], last)
    return (grad_input, result["down"][None])


def far_device(dy_values, dy_scales, expert_ids, saved_pre, w_gate, w_up, w_down):
    groups, width = lax.axis_size("expert"), w_down.shape[2]
    slots = saved_pre.shape[0]
    cap = slots // groups
    route = expert_ids[:, 0]
    rows, count = route.shape[0], dy_scales.shape[1]
    onehot = (route[:, None] == jnp.arange(groups, dtype=jnp.int32)[None, :]).astype(BF16)
    earlier = jnp.dot(jnp.tri(rows, k=-1, dtype=BF16), onehot, preferred_element_type=F32)
    rank = jnp.sum(earlier * onehot.astype(F32), axis=1).astype(jnp.int32)
    place = route * cap + rank
    chosen = (place[:, None] == jnp.arange(slots, dtype=jnp.int32)[None, :]).astype(BF16)
    scaled = dy_values.astype(F32).reshape(rows, count, -1) * dy_scales.astype(F32)[:, :, None]
    scaled = scaled.reshape(dy_values.shape).astype(BF16)
    packed = lax.dot_general(chosen, scaled, BY_ROWS, preferred_element_type=F32).astype(BF16)
    received = lax.all_to_all(packed, "expert", split_axis=0, concat_axis=0, tiled=True)
    gate, up, sigmoid = swish_parts(saved_pre, width)
    hidden = (gate * sigmoid * up).astype(BF16)
    partial = jnp.dot(received, w_down[0], preferred_element_type=F32)
    grad = lax.psum(partial, "dp")
    d_gate = (grad * up * sigmoid * (1.0 + gate * (1.0 - sigmoid))).astype(BF16)
    d_up = (grad * (gate * sigmoid)).astype(BF16)
    result = lax.dot_general(d_gate, w_gate[0], TRANSPOSED, preferred_element_type=F32)
    result += lax.dot_general(d_up, w_up[0], TRANSPOSED, preferred_element_type=F32)
    returned = lax.all_to_all(
        result.astype(BF16), "expert", split_axis=0, concat_axis=0, tiled=True
    )
    grad_input = jnp.dot(chosen, returned, preferred_element_type=F32).astype(BF16)
    grad_down = lax.dot_general(received, hidden, BY_ROWS, preferred_element_type=F32)
    return (grad_input, grad_down[None])


def solution(mesh):
    near = mesh.shape["expert"] == 8 and mesh.shape["dp"] == 4
    return jax.shard_map(
        near_device if near else far_device,
        mesh=mesh,
        in_specs=(
            P("expert", "dp"),
            P("expert", "dp"),
            P("expert", None),
            P("expert", None),
            P("expert", "dp", None),
            P("expert", "dp", None),
            P("expert", "dp", None),
        ),
        out_specs=(P("expert", "dp"), P("expert", "dp", None)),
        check_vma=False,
    )
```

```python
import functools

import jax
import jax.numpy as jnp
from jax import lax
from jax.experimental import pallas as pl
from jax.experimental.pallas import tpu as pltpu
from jax.sharding import PartitionSpec as P

CHUNKS = ((0, 1), (6, 7), (2, 4), (3, 5))
LATER = (2, 4, 3, 5, 0)
PARTS = (CHUNKS[2], CHUNKS[0] + CHUNKS[1], CHUNKS[3])
ORDER = (
    ("first", 0), ("diagonal", 0), ("add", 0), ("prep", 0), ("turn", 0), ("first", 1),
    ("first", 2), ("add", 0), ("add", 1), ("first", 3), ("add", 2), ("add", 1), ("add", 3),
    ("down", 0), ("add", 2), ("second", 1), ("add", 3), ("release", 0), ("second", 2),
    ("second", 3), ("second", 0), ("cross", 0), ("gather", 0), ("gather", 1),
)
HELD = (0,)
COST = {
    "place": 10**10, "pack": 10**10, "rest": 1, "first": 1, "prep": 1, "turn": 1,
    "add": 10**9, "release": 1, "pair": 1, "second": 10**10, "down": 1, "gather": 5 * 10**9, "finish": 1,
}
MIB = 1 << 20
BF16, F32 = jnp.bfloat16, jnp.float32
TRANSPOSED = (((1,), (1,)), ((), ()))
BY_ROWS = (((0,), (0,)), ((), ()))


VMEM, HBM, ANY = (
    pl.BlockSpec(memory_space=space) for space in (pltpu.VMEM, pltpu.HBM, pl.ANY)
)


def call(body, name, operands, specs, outs, out_specs, vmem=16, scratch=(), after=()):
    count, waits = len(operands), len(after)

    def run(*refs):
        body(*refs[:count], *refs[count + waits :])

    return pl.pallas_call(
        run,
        name=name,
        out_shape=outs,
        in_specs=list(specs) + [ANY] * waits,
        out_specs=out_specs,
        scratch_shapes=scratch,
        compiler_params=pltpu.CompilerParams(vmem_limit_bytes=vmem * MIB),
        cost_estimate=pl.CostEstimate(flops=COST[name], bytes_accessed=0, transcendentals=0),
    )(*operands, *after)


def in_hbm(array):
    return pltpu.with_memory_space_constraint(array, pltpu.HBM)


def swish_parts(pre, width):
    gate, up = pre[:, :width].astype(F32), pre[:, width:].astype(F32)
    sigmoid = jax.nn.sigmoid(gate)
    return gate, up, sigmoid


def tiles(size):
    step = 256 if size % 256 == 0 else size
    return [slice(i, i + step) for i in range(0, size, step)]


def arrays_of(blocks):
    found = []
    for array, _ in blocks:
        if not any(array is other for other in found):
            found.append(array)
    return found


def spots_of(blocks, arrays):
    return [(next(i for i, x in enumerate(arrays) if x is array), row) for array, row in blocks]


def rows_at(refs, spots, cap):
    return jnp.concatenate([refs[i][row : row + cap] for i, row in spots], axis=0)


def place_body(groups, cap, ids, place, ids_in, sems):
    bring = pltpu.make_async_copy(ids, ids_in, sems.at[0])
    bring.start()
    rows, slots, lines = ids.shape[1], groups * cap, max(8, groups)
    line = lax.broadcasted_iota(jnp.int32, (lines, rows), 0)
    sooner = lax.broadcasted_iota(jnp.int32, (rows, rows), 0)
    later = lax.broadcasted_iota(jnp.int32, (rows, rows), 1)
    before = jnp.where(sooner < later, 1.0, 0.0).astype(BF16)
    bring.wait()
    route = ids_in[...]
    onehot = jnp.where(line == route, 1.0, 0.0)
    earlier = jnp.dot(onehot.astype(BF16), before, preferred_element_type=F32)
    rank = jnp.sum(earlier * onehot, axis=0, keepdims=True).astype(jnp.int32)
    position = (route ^ lax.axis_index("expert")) * cap + rank
    slot = lax.broadcasted_iota(jnp.int32, (slots, rows), 0)
    place[...] = jnp.where(slot == position, 1.0, 0.0).astype(BF16)


def find_place(ids, groups, cap):
    rows = ids.shape[0]
    return call(
        functools.partial(place_body, groups, cap),
        "place",
        (in_hbm(ids.T),),
        (HBM,),
        [jax.ShapeDtypeStruct((groups * cap, rows), BF16)],
        [VMEM],
        16,
        [pltpu.VMEM((1, rows), jnp.int32), pltpu.SemaphoreType.DMA((1,))],
    )[0]


def put_blocks(place, rows, outs, groups, cap):
    chosen = rows_at([place], [(0, k * cap) for group in groups for k in group], cap)
    for part in tiles(rows.shape[1]):
        packed = jnp.dot(chosen, rows[:, part], preferred_element_type=F32).astype(BF16)
        start = 0
        for group, out in zip(groups, outs):
            out[:, part] = packed[start : start + len(group) * cap]
            start += len(group) * cap


def pack_body(groups, cap, place, scales, values, scaled, *outs):
    features, count = values.shape[1], scales.shape[0]
    owner = lax.broadcasted_iota(jnp.int32, (count, features), 1) // (features // count)
    spread = jnp.where(owner == lax.broadcasted_iota(jnp.int32, (count, features), 0), 1.0, 0.0)
    spread = spread.astype(BF16)
    for part in tiles(features):
        factor = lax.dot_general(
            scales[...], spread[:, part], BY_ROWS, preferred_element_type=F32
        )
        scaled[:, part] = (values[:, part].astype(F32) * factor).astype(BF16)
    put_blocks(place, scaled, outs, groups, cap)


def rest_body(groups, cap, place, scaled, *outs):
    put_blocks(place, scaled, outs, groups, cap)


def pack(place, values, scales, groups, cap):
    rows, features = values.shape
    return call(
        functools.partial(pack_body, groups, cap),
        "pack",
        (place, scales.T, values),
        [VMEM] * 3,
        [jax.ShapeDtypeStruct((rows, features), BF16)]
        + [jax.ShapeDtypeStruct((len(group) * cap, features), BF16) for group in groups],
        [VMEM] * (1 + len(groups)),
    )


def pack_rest(place, scaled, groups, cap, after):
    features = scaled.shape[1]
    return call(
        functools.partial(rest_body, groups, cap),
        "rest",
        (place, scaled),
        [VMEM] * 2,
        [jax.ShapeDtypeStruct((len(group) * cap, features), BF16) for group in groups],
        [VMEM] * len(groups),
        after=after,
    )


def pair_body(count, spots, cap, *refs):
    refs[count][...] = rows_at(refs[:count], spots, cap)


def pair(blocks, cap, after):
    arrays = arrays_of(blocks)
    shape = jax.ShapeDtypeStruct((len(blocks) * cap, arrays[0].shape[1]), BF16)
    return call(
        functools.partial(pair_body, len(arrays), spots_of(blocks, arrays), cap),
        "pair",
        arrays,
        [VMEM] * len(arrays),
        [shape],
        [VMEM],
        after=after,
    )[0]


def first_body(count, spots, cap, weight, *refs):
    arrays, send, keep, both = refs[:count], *refs[count:]
    rows = rows_at(arrays, spots, cap)
    width = weight.shape[1]
    for part in tiles(width):
        both[:, part] = jnp.dot(rows, weight[:, part], preferred_element_type=F32)
    halves = [slice(0, width // 2), slice(width // 2, width)]
    for odd, (theirs, mine) in enumerate((reversed(halves), halves)):

        @pl.when(lax.axis_index("dp") % 2 == odd)
        def _():
            send[...] = both[:, theirs].astype(BF16)
            keep[...] = both[:, mine]


def first(blocks, weight, cap, after):
    arrays = arrays_of(blocks)
    features, width = weight.shape
    size = len(blocks) * cap
    return call(
        functools.partial(first_body, len(arrays), spots_of(blocks, arrays), cap),
        "first",
        (weight, *arrays),
        [VMEM] * (1 + len(arrays)),
        [jax.ShapeDtypeStruct((size, width // 2), dtype) for dtype in (BF16, F32)],
        [VMEM] * 2,
        16,
        [pltpu.VMEM((size, width), F32)],
        after=after,
    )


def add_body(count, keep, *refs):
    total = keep[...]
    for got in refs[:count]:
        total = total + got[...].astype(F32)
    refs[count][...] = total.astype(BF16)


def add(keep, gots, after):
    return call(
        functools.partial(add_body, len(gots)),
        "add",
        (keep, *gots),
        [VMEM] * (1 + len(gots)),
        [jax.ShapeDtypeStruct(keep.shape, BF16)],
        [VMEM],
        16,
        after=after,
    )[0]


def release_body(total, out):
    out[...] = total[...]


def release(total, after):
    shape = jax.ShapeDtypeStruct(total.shape, total.dtype)
    return call(release_body, "release", (total,), [VMEM], [shape], [VMEM], after=after)[0]


def prep_body(saved, gate_factor, up_factor, hidden):
    slots, width = hidden.shape
    step = 32 if slots % 32 == 0 else slots

    def some(i, carry):
        at = pl.ds(pl.multiple_of(i * step, step), step)
        gate, up, sigmoid = swish_parts(saved[at, :], width)
        silu = gate * sigmoid
        gate_factor[at, :] = up * sigmoid * (1.0 + gate * (1.0 - sigmoid))
        up_factor[at, :] = silu
        hidden[at, :] = (silu * up).astype(BF16)
        return carry

    lax.fori_loop(0, slots // step, some, 0)


def prep(saved_pre, after):
    slots, width = saved_pre.shape[0], saved_pre.shape[1] // 2
    return call(
        prep_body,
        "prep",
        (saved_pre,),
        [VMEM],
        [jax.ShapeDtypeStruct((slots, width), dtype) for dtype in (F32, F32, BF16)],
        [VMEM] * 3,
        16,
        after=after,
    )


def turn_body(count, cap, groups, place, *refs):
    weights, turned, places = refs[:count], refs[count : 2 * count], refs[2 * count :]
    for weight, out in zip(weights, turned):
        for part in tiles(weight.shape[0]):
            out[:, part] = weight[part, :].T
    for group, out in zip(groups, places):
        out[...] = rows_at([place], [(0, k * cap) for k in group], cap).T


def turn(weights, place, groups, cap, after):
    count, rows = len(weights), place.shape[1]
    return call(
        functools.partial(turn_body, count, cap, groups),
        "turn",
        (place, *weights),
        [VMEM] * (1 + count),
        [jax.ShapeDtypeStruct(x.shape[::-1], x.dtype) for x in weights]
        + [jax.ShapeDtypeStruct((rows, len(group) * cap), BF16) for group in groups],
        [VMEM] * (count + len(groups)),
        16,
        after=after,
    )


def slots_of(ref, k, cap):
    start = pl.multiple_of((lax.axis_index("expert") ^ k) * cap, cap)
    return ref[pl.ds(start, cap), :]


def second_body(chunk, cap, own, other, gate_factor, up_factor, w_gate, w_up, *refs):
    outs, grads = refs[:-1], refs[-1]
    width, features = w_gate.shape
    halves = [slice(0, width // 2), slice(width // 2, width)]
    for odd, (theirs, mine) in enumerate((reversed(halves), halves)):

        @pl.when(lax.axis_index("dp") % 2 == odd)
        def _():
            grads[:, mine] = own[...]
            grads[:, theirs] = other[...]

    grad = grads[...].astype(F32)
    d_gate, d_up = (
        (grad * jnp.concatenate([slots_of(factor, k, cap) for k in chunk], axis=0))
        .astype(BF16)
        for factor in (gate_factor, up_factor)
    )
    for part in tiles(features):
        result = jnp.dot(d_gate, w_gate[:, part], preferred_element_type=F32)
        result += jnp.dot(d_up, w_up[:, part], preferred_element_type=F32)
        result = result.astype(BF16)
        size = result.shape[0] // len(outs)
        for i, out in enumerate(outs):
            out[:, part] = result[i * size : (i + 1) * size]


def second(own, other, factors, weights, chunk, cap, together, after):
    width, features = weights[0].shape
    count = 1 if together else len(chunk)
    size = len(chunk) // count * cap
    return call(
        functools.partial(second_body, chunk, cap),
        "second",
        (own, other, *factors, *weights),
        [VMEM] * 6,
        [jax.ShapeDtypeStruct((size, features), BF16)] * count,
        [VMEM] * count,
        24,
        [pltpu.VMEM((len(chunk) * cap, width), BF16)],
        after=after,
    )


def down_body(count, spots, hidden, *refs):
    arrays, out, flag, sums, sems = refs[:count], *refs[count:]
    flag[...] = jnp.zeros_like(flag)
    cap = hidden.shape[0] // len(spots)
    features, width = out.shape
    mine = jnp.concatenate([slots_of(hidden, k, cap) for k in range(len(spots))], axis=0)
    tile = sums.shape[1]
    copies = []
    for i in range(features // tile):
        part = [arrays[a][row : row + cap, i * tile : (i + 1) * tile] for a, row in spots]
        part = jnp.concatenate(part, axis=0)
        sums[i] = lax.dot_general(part, mine, BY_ROWS, preferred_element_type=F32)
        copies.append(
            pltpu.make_async_copy(sums.at[i], out.at[pl.ds(i * tile, tile)], sems.at[i])
        )
        copies[-1].start()
    for copy in copies:
        copy.wait()


def down(blocks, hidden, features, after):
    arrays = arrays_of(blocks)
    slots, width = hidden.shape
    tile = min(features, 256)
    steps = features // tile
    return call(
        functools.partial(down_body, len(arrays), spots_of(blocks, arrays)),
        "down",
        (hidden, *arrays),
        [VMEM] * (1 + len(arrays)),
        [jax.ShapeDtypeStruct((features, width), F32), jax.ShapeDtypeStruct((8, 128), F32)],
        [HBM, VMEM],
        24,
        [pltpu.VMEM((steps, tile, width), F32), pltpu.SemaphoreType.DMA((steps,))],
        after=after,
    )


def rows_of(place, arrays, spots, cap, part):
    returned = [arrays[i][row : row + cap, part] for i, row in spots]
    returned = jnp.concatenate(returned, axis=0)
    return jnp.dot(place[...], returned, preferred_element_type=F32).astype(BF16)


def gather_body(count, spots, cap, place, *refs):
    arrays, sooner, out = refs[:count], refs[count:-1], refs[-1]
    for part in tiles(out.shape[1]):
        rows = rows_of(place, arrays, spots, cap, part)
        for others in sooner:
            rows += others[:, part]
        out[:, part] = rows


def gather(place, blocks, cap, sooner, after):
    arrays = arrays_of(blocks)
    rows, features = place.shape[0], arrays[0].shape[1]
    return call(
        functools.partial(gather_body, len(arrays), spots_of(blocks, arrays), cap),
        "gather",
        (place, *arrays, *sooner),
        [VMEM] * (1 + len(arrays) + len(sooner)),
        [jax.ShapeDtypeStruct((rows, features), BF16)],
        [VMEM],
        16,
        after=after,
    )[0]


def finish_body(count, spots, cap, place, sooner, *refs):
    arrays, out, whole, sems = refs[:count], *refs[count:]
    copies = []
    for i, part in enumerate(tiles(out.shape[1])):
        whole[:, part] = rows_of(place, arrays, spots, cap, part) + sooner[:, part]
        copies.append(pltpu.make_async_copy(whole.at[:, part], out.at[:, part], sems.at[i]))
        copies[-1].start()
    for copy in copies:
        copy.wait()


def finish(place, blocks, cap, sooner, after):
    arrays, (rows, features) = arrays_of(blocks), sooner.shape
    return call(
        functools.partial(finish_body, len(arrays), spots_of(blocks, arrays), cap),
        "finish",
        (place, sooner, *arrays),
        [VMEM] * (2 + len(arrays)),
        [jax.ShapeDtypeStruct((rows, features), BF16)],
        [HBM],
        16,
        [
            pltpu.VMEM((rows, features), BF16),
            pltpu.SemaphoreType.DMA((len(tiles(features)),)),
        ],
        after=after,
    )[0]


def swap(block, axis, k):
    size = lax.axis_size(axis)
    return lax.ppermute(block, axis, [(i, i ^ k) for i in range(size)])


def near_device(dy_values, dy_scales, expert_ids, saved_pre, w_gate, w_up, w_down):
    groups = lax.axis_size("expert")
    cap = saved_pre.shape[0] // groups
    features = dy_values.shape[1]
    keeps, gots, owns, others, returned, result = {}, {}, {}, {}, {}, {}

    place = find_place(expert_ids, groups, cap)
    last, sooner = [place], []
    scaled, crossing, ahead = pack(place, dy_values, dy_scales, ((1, 7), (6,)), cap)
    side = swap(crossing, "expert", 1)
    rest = pack_rest(place, scaled, [(k,) for k in LATER], cap, [crossing])
    last[:] = rest[-1:]
    blocks = {1: (side, 0)}
    for k, block in zip(LATER, rest):
        blocks[k] = (swap(block, "expert", k) if k else block, 0)

    def do_diagonal(_):
        both = pair([(ahead, 0), (side, cap)], cap, last)
        last[:] = [both]
        got = swap(both, "expert", 6)
        blocks.update({6: (got, 0), 7: (got, cap)})

    def do_first(c):
        send, keeps[c] = first([blocks[k] for k in CHUNKS[c]], w_down[0], cap, last)
        last[:] = [send]
        gots[c] = [swap(send, "dp", 1)]

    def do_add(c):
        part = add(keeps[c], gots[c], last)
        last[:] = [part]
        if len(gots[c]) == 1:
            gots[c].append(swap(part, "dp", 2))
        elif c in HELD:
            owns[c] = part
        else:
            owns[c], others[c] = part, swap(part, "dp", 1)

    def do_release(c):
        owns[c] = release(owns[c], last)
        last[:] = [owns[c]]
        others[c] = swap(owns[c], "dp", 1)

    def do_prep(_):
        *result["factors"], result["hidden"] = prep(saved_pre, last)
        last[:] = [result["hidden"]]

    def do_turn(_):
        turned = turn((w_gate[0], w_up[0]), place, PARTS, cap, last)
        result["weights"], result["places"] = turned[:2], turned[2:]
        last[:] = turned[:1]

    def do_second(c):
        chunk = CHUNKS[c]
        grads = second(
            owns[c], others[c], result["factors"], result["weights"], chunk, cap, 6 in chunk, last
        )
        last[:] = [grads[0]]
        if 6 in chunk:
            result["back"] = swap(grads[0], "expert", 6)
            returned[6] = (result["back"], 0)
        elif 0 in chunk:
            returned[0], result["near"] = (grads[0], 0), grads[1]
        else:
            returned.update({k: (swap(grad, "expert", k), 0) for k, grad in zip(chunk, grads)})

    def do_cross(_):
        both = pair([(result["near"], 0), (result["back"], cap)], cap, last)
        last[:] = [both]
        got = swap(both, "expert", 1)
        returned.update({1: (got, 0), 7: (got, cap)})

    def do_down(_):
        every = [blocks[k] for k in range(groups)]
        result["down"], flag = down(every, result["hidden"], features, last)
        last[:] = [flag]

    def do_gather(part):
        came = [returned[k] for k in PARTS[part]]
        sooner[:] = [gather(result["places"][part], came, cap, sooner, last)]
        last[:] = sooner

    steps = {
        "first": do_first,
        "add": do_add,
        "release": do_release,
        "diagonal": do_diagonal,
        "cross": do_cross,
        "prep": do_prep,
        "turn": do_turn,
        "second": do_second,
        "down": do_down,
        "gather": do_gather,
    }
    for step, c in ORDER:
        steps[step](c)
    came = [returned[k] for k in PARTS[-1]]
    grad_input = finish(result["places"][-1], came, cap, sooner[0], last)
    return (grad_input, result["down"][None])


def far_device(dy_values, dy_scales, expert_ids, saved_pre, w_gate, w_up, w_down):
    groups, width = lax.axis_size("expert"), w_down.shape[2]
    slots = saved_pre.shape[0]
    cap = slots // groups
    route = expert_ids[:, 0]
    rows, count = route.shape[0], dy_scales.shape[1]
    onehot = (route[:, None] == jnp.arange(groups, dtype=jnp.int32)[None, :]).astype(BF16)
    earlier = jnp.dot(jnp.tri(rows, k=-1, dtype=BF16), onehot, preferred_element_type=F32)
    rank = jnp.sum(earlier * onehot.astype(F32), axis=1).astype(jnp.int32)
    place = route * cap + rank
    chosen = (place[:, None] == jnp.arange(slots, dtype=jnp.int32)[None, :]).astype(BF16)
    scaled = dy_values.astype(F32).reshape(rows, count, -1) * dy_scales.astype(F32)[:, :, None]
    scaled = scaled.reshape(dy_values.shape).astype(BF16)
    packed = lax.dot_general(chosen, scaled, BY_ROWS, preferred_element_type=F32).astype(BF16)
    received = lax.all_to_all(packed, "expert", split_axis=0, concat_axis=0, tiled=True)
    gate, up, sigmoid = swish_parts(saved_pre, width)
    hidden = (gate * sigmoid * up).astype(BF16)
    partial = jnp.dot(received, w_down[0], preferred_element_type=F32)
    grad = lax.psum(partial, "dp")
    d_gate = (grad * up * sigmoid * (1.0 + gate * (1.0 - sigmoid))).astype(BF16)
    d_up = (grad * (gate * sigmoid)).astype(BF16)
    result = lax.dot_general(d_gate, w_gate[0], TRANSPOSED, preferred_element_type=F32)
    result += lax.dot_general(d_up, w_up[0], TRANSPOSED, preferred_element_type=F32)
    returned = lax.all_to_all(
        result.astype(BF16), "expert", split_axis=0, concat_axis=0, tiled=True
    )
    grad_input = jnp.dot(chosen, returned, preferred_element_type=F32).astype(BF16)
    grad_down = lax.dot_general(received, hidden, BY_ROWS, preferred_element_type=F32)
    return (grad_input, grad_down[None])


def solution(mesh):
    near = mesh.shape["expert"] == 8 and mesh.shape["dp"] == 4
    return jax.shard_map(
        near_device if near else far_device,
        mesh=mesh,
        in_specs=(
            P("expert", "dp"),
            P("expert", "dp"),
            P("expert", None),
            P("expert", None),
            P("expert", "dp", None),
            P("expert", "dp", None),
            P("expert", "dp", None),
        ),
        out_specs=(P("expert", "dp"), P("expert", "dp", None)),
        check_vma=False,
    )
```

```python
import functools

import jax
import jax.numpy as jnp
from jax import lax
from jax.experimental import pallas as pl
from jax.experimental.pallas import tpu as pltpu
from jax.sharding import PartitionSpec as P

CHUNKS = ((0, 1), (6, 7), (2, 4), (3, 5))
LATER = (2, 4, 3, 5, 0)
PARTS = (CHUNKS[2], CHUNKS[0] + CHUNKS[1], CHUNKS[3])
ORDER = (
    ("first", 0), ("diagonal", 0), ("add", 0), ("prep", 0), ("turn", 0), ("first", 1),
    ("first", 2), ("add", 0), ("add", 1), ("first", 3), ("add", 2), ("add", 1), ("add", 3),
    ("release", 0), ("down", 0), ("add", 2), ("second", 1), ("second", 0), ("add", 3),
    ("second", 2), ("second", 3), ("cross", 0), ("gather", 0), ("gather", 1),
)
HELD = (0,)
COST = {
    "place": 10**10, "pack": 10**10, "rest": 1, "first": 1, "prep": 1, "turn": 1,
    "add": 10**9, "release": 1, "pair": 1, "second": 10**10, "down": 1, "gather": 5 * 10**9, "finish": 1,
}
MIB = 1 << 20
BF16, F32 = jnp.bfloat16, jnp.float32
TRANSPOSED = (((1,), (1,)), ((), ()))
BY_ROWS = (((0,), (0,)), ((), ()))


VMEM, HBM, ANY = (
    pl.BlockSpec(memory_space=space) for space in (pltpu.VMEM, pltpu.HBM, pl.ANY)
)


def call(body, name, operands, specs, outs, out_specs, vmem=16, scratch=(), after=()):
    count, waits = len(operands), len(after)

    def run(*refs):
        body(*refs[:count], *refs[count + waits :])

    return pl.pallas_call(
        run,
        name=name,
        out_shape=outs,
        in_specs=list(specs) + [ANY] * waits,
        out_specs=out_specs,
        scratch_shapes=scratch,
        compiler_params=pltpu.CompilerParams(vmem_limit_bytes=vmem * MIB),
        cost_estimate=pl.CostEstimate(flops=COST[name], bytes_accessed=0, transcendentals=0),
    )(*operands, *after)


def in_hbm(array):
    return pltpu.with_memory_space_constraint(array, pltpu.HBM)


def swish_parts(pre, width):
    gate, up = pre[:, :width].astype(F32), pre[:, width:].astype(F32)
    sigmoid = jax.nn.sigmoid(gate)
    return gate, up, sigmoid


def tiles(size):
    step = 256 if size % 256 == 0 else size
    return [slice(i, i + step) for i in range(0, size, step)]


def arrays_of(blocks):
    found = []
    for array, _ in blocks:
        if not any(array is other for other in found):
            found.append(array)
    return found


def spots_of(blocks, arrays):
    return [(next(i for i, x in enumerate(arrays) if x is array), row) for array, row in blocks]


def rows_at(refs, spots, cap):
    return jnp.concatenate([refs[i][row : row + cap] for i, row in spots], axis=0)


def place_body(groups, cap, ids, place, ids_in, sems):
    bring = pltpu.make_async_copy(ids, ids_in, sems.at[0])
    bring.start()
    rows, slots, lines = ids.shape[1], groups * cap, max(8, groups)
    line = lax.broadcasted_iota(jnp.int32, (lines, rows), 0)
    sooner = lax.broadcasted_iota(jnp.int32, (rows, rows), 0)
    later = lax.broadcasted_iota(jnp.int32, (rows, rows), 1)
    before = jnp.where(sooner < later, 1.0, 0.0).astype(BF16)
    bring.wait()
    route = ids_in[...]
    onehot = jnp.where(line == route, 1.0, 0.0)
    earlier = jnp.dot(onehot.astype(BF16), before, preferred_element_type=F32)
    rank = jnp.sum(earlier * onehot, axis=0, keepdims=True).astype(jnp.int32)
    position = (route ^ lax.axis_index("expert")) * cap + rank
    slot = lax.broadcasted_iota(jnp.int32, (slots, rows), 0)
    place[...] = jnp.where(slot == position, 1.0, 0.0).astype(BF16)


def find_place(ids, groups, cap):
    rows = ids.shape[0]
    return call(
        functools.partial(place_body, groups, cap),
        "place",
        (in_hbm(ids.T),),
        (HBM,),
        [jax.ShapeDtypeStruct((groups * cap, rows), BF16)],
        [VMEM],
        16,
        [pltpu.VMEM((1, rows), jnp.int32), pltpu.SemaphoreType.DMA((1,))],
    )[0]


def put_blocks(place, rows, outs, groups, cap):
    chosen = rows_at([place], [(0, k * cap) for group in groups for k in group], cap)
    for part in tiles(rows.shape[1]):
        packed = jnp.dot(chosen, rows[:, part], preferred_element_type=F32).astype(BF16)
        start = 0
        for group, out in zip(groups, outs):
            out[:, part] = packed[start : start + len(group) * cap]
            start += len(group) * cap


def pack_body(groups, cap, place, scales, values, scaled, *outs):
    features, count = values.shape[1], scales.shape[0]
    owner = lax.broadcasted_iota(jnp.int32, (count, features), 1) // (features // count)
    spread = jnp.where(owner == lax.broadcasted_iota(jnp.int32, (count, features), 0), 1.0, 0.0)
    spread = spread.astype(BF16)
    for part in tiles(features):
        factor = lax.dot_general(
            scales[...], spread[:, part], BY_ROWS, preferred_element_type=F32
        )
        scaled[:, part] = (values[:, part].astype(F32) * factor).astype(BF16)
    put_blocks(place, scaled, outs, groups, cap)


def rest_body(groups, cap, place, scaled, *outs):
    put_blocks(place, scaled, outs, groups, cap)


def pack(place, values, scales, groups, cap):
    rows, features = values.shape
    return call(
        functools.partial(pack_body, groups, cap),
        "pack",
        (place, scales.T, values),
        [VMEM] * 3,
        [jax.ShapeDtypeStruct((rows, features), BF16)]
        + [jax.ShapeDtypeStruct((len(group) * cap, features), BF16) for group in groups],
        [VMEM] * (1 + len(groups)),
    )


def pack_rest(place, scaled, groups, cap, after):
    features = scaled.shape[1]
    return call(
        functools.partial(rest_body, groups, cap),
        "rest",
        (place, scaled),
        [VMEM] * 2,
        [jax.ShapeDtypeStruct((len(group) * cap, features), BF16) for group in groups],
        [VMEM] * len(groups),
        after=after,
    )


def pair_body(count, spots, cap, *refs):
    refs[count][...] = rows_at(refs[:count], spots, cap)


def pair(blocks, cap, after):
    arrays = arrays_of(blocks)
    shape = jax.ShapeDtypeStruct((len(blocks) * cap, arrays[0].shape[1]), BF16)
    return call(
        functools.partial(pair_body, len(arrays), spots_of(blocks, arrays), cap),
        "pair",
        arrays,
        [VMEM] * len(arrays),
        [shape],
        [VMEM],
        after=after,
    )[0]


def first_body(count, spots, cap, weight, *refs):
    arrays, send, keep, both = refs[:count], *refs[count:]
    rows = rows_at(arrays, spots, cap)
    width = weight.shape[1]
    for part in tiles(width):
        both[:, part] = jnp.dot(rows, weight[:, part], preferred_element_type=F32)
    halves = [slice(0, width // 2), slice(width // 2, width)]
    for odd, (theirs, mine) in enumerate((reversed(halves), halves)):

        @pl.when(lax.axis_index("dp") % 2 == odd)
        def _():
            send[...] = both[:, theirs].astype(BF16)
            keep[...] = both[:, mine]


def first(blocks, weight, cap, after):
    arrays = arrays_of(blocks)
    features, width = weight.shape
    size = len(blocks) * cap
    return call(
        functools.partial(first_body, len(arrays), spots_of(blocks, arrays), cap),
        "first",
        (weight, *arrays),
        [VMEM] * (1 + len(arrays)),
        [jax.ShapeDtypeStruct((size, width // 2), dtype) for dtype in (BF16, F32)],
        [VMEM] * 2,
        16,
        [pltpu.VMEM((size, width), F32)],
        after=after,
    )


def add_body(count, keep, *refs):
    total = keep[...]
    for got in refs[:count]:
        total = total + got[...].astype(F32)
    refs[count][...] = total.astype(BF16)


def add(keep, gots, after):
    return call(
        functools.partial(add_body, len(gots)),
        "add",
        (keep, *gots),
        [VMEM] * (1 + len(gots)),
        [jax.ShapeDtypeStruct(keep.shape, BF16)],
        [VMEM],
        16,
        after=after,
    )[0]


def release_body(total, out):
    out[...] = total[...]


def release(total, after):
    shape = jax.ShapeDtypeStruct(total.shape, total.dtype)
    return call(release_body, "release", (total,), [VMEM], [shape], [VMEM], after=after)[0]


def prep_body(saved, gate_factor, up_factor, hidden):
    slots, width = hidden.shape
    step = 32 if slots % 32 == 0 else slots

    def some(i, carry):
        at = pl.ds(pl.multiple_of(i * step, step), step)
        gate, up, sigmoid = swish_parts(saved[at, :], width)
        silu = gate * sigmoid
        gate_factor[at, :] = up * sigmoid * (1.0 + gate * (1.0 - sigmoid))
        up_factor[at, :] = silu
        hidden[at, :] = (silu * up).astype(BF16)
        return carry

    lax.fori_loop(0, slots // step, some, 0)


def prep(saved_pre, after):
    slots, width = saved_pre.shape[0], saved_pre.shape[1] // 2
    return call(
        prep_body,
        "prep",
        (saved_pre,),
        [VMEM],
        [jax.ShapeDtypeStruct((slots, width), dtype) for dtype in (F32, F32, BF16)],
        [VMEM] * 3,
        16,
        after=after,
    )


def turn_body(count, cap, groups, place, *refs):
    weights, turned, places = refs[:count], refs[count : 2 * count], refs[2 * count :]
    for weight, out in zip(weights, turned):
        for part in tiles(weight.shape[0]):
            out[:, part] = weight[part, :].T
    for group, out in zip(groups, places):
        out[...] = rows_at([place], [(0, k * cap) for k in group], cap).T


def turn(weights, place, groups, cap, after):
    count, rows = len(weights), place.shape[1]
    return call(
        functools.partial(turn_body, count, cap, groups),
        "turn",
        (place, *weights),
        [VMEM] * (1 + count),
        [jax.ShapeDtypeStruct(x.shape[::-1], x.dtype) for x in weights]
        + [jax.ShapeDtypeStruct((rows, len(group) * cap), BF16) for group in groups],
        [VMEM] * (count + len(groups)),
        16,
        after=after,
    )


def slots_of(ref, k, cap):
    start = pl.multiple_of((lax.axis_index("expert") ^ k) * cap, cap)
    return ref[pl.ds(start, cap), :]


def second_body(chunk, cap, own, other, gate_factor, up_factor, w_gate, w_up, *refs):
    outs, grads = refs[:-1], refs[-1]
    width, features = w_gate.shape
    halves = [slice(0, width // 2), slice(width // 2, width)]
    for odd, (theirs, mine) in enumerate((reversed(halves), halves)):

        @pl.when(lax.axis_index("dp") % 2 == odd)
        def _():
            grads[:, mine] = own[...]
            grads[:, theirs] = other[...]

    grad = grads[...].astype(F32)
    d_gate, d_up = (
        (grad * jnp.concatenate([slots_of(factor, k, cap) for k in chunk], axis=0))
        .astype(BF16)
        for factor in (gate_factor, up_factor)
    )
    for part in tiles(features):
        result = jnp.dot(d_gate, w_gate[:, part], preferred_element_type=F32)
        result += jnp.dot(d_up, w_up[:, part], preferred_element_type=F32)
        result = result.astype(BF16)
        size = result.shape[0] // len(outs)
        for i, out in enumerate(outs):
            out[:, part] = result[i * size : (i + 1) * size]


def second(own, other, factors, weights, chunk, cap, together, after):
    width, features = weights[0].shape
    count = 1 if together else len(chunk)
    size = len(chunk) // count * cap
    return call(
        functools.partial(second_body, chunk, cap),
        "second",
        (own, other, *factors, *weights),
        [VMEM] * 6,
        [jax.ShapeDtypeStruct((size, features), BF16)] * count,
        [VMEM] * count,
        24,
        [pltpu.VMEM((len(chunk) * cap, width), BF16)],
        after=after,
    )


def down_body(count, spots, hidden, *refs):
    arrays, out, flag, sums, sems = refs[:count], *refs[count:]
    flag[...] = jnp.zeros_like(flag)
    cap = hidden.shape[0] // len(spots)
    features, width = out.shape
    mine = jnp.concatenate([slots_of(hidden, k, cap) for k in range(len(spots))], axis=0)
    tile = sums.shape[1]
    copies = []
    for i in range(features // tile):
        part = [arrays[a][row : row + cap, i * tile : (i + 1) * tile] for a, row in spots]
        part = jnp.concatenate(part, axis=0)
        sums[i] = lax.dot_general(part, mine, BY_ROWS, preferred_element_type=F32)
        copies.append(
            pltpu.make_async_copy(sums.at[i], out.at[pl.ds(i * tile, tile)], sems.at[i])
        )
        copies[-1].start()
    for copy in copies:
        copy.wait()


def down(blocks, hidden, features, after):
    arrays = arrays_of(blocks)
    slots, width = hidden.shape
    tile = min(features, 256)
    steps = features // tile
    return call(
        functools.partial(down_body, len(arrays), spots_of(blocks, arrays)),
        "down",
        (hidden, *arrays),
        [VMEM] * (1 + len(arrays)),
        [jax.ShapeDtypeStruct((features, width), F32), jax.ShapeDtypeStruct((8, 128), F32)],
        [HBM, VMEM],
        24,
        [pltpu.VMEM((steps, tile, width), F32), pltpu.SemaphoreType.DMA((steps,))],
        after=after,
    )


def rows_of(place, arrays, spots, cap, part):
    returned = [arrays[i][row : row + cap, part] for i, row in spots]
    returned = jnp.concatenate(returned, axis=0)
    return jnp.dot(place[...], returned, preferred_element_type=F32).astype(BF16)


def gather_body(count, spots, cap, place, *refs):
    arrays, sooner, out = refs[:count], refs[count:-1], refs[-1]
    for part in tiles(out.shape[1]):
        rows = rows_of(place, arrays, spots, cap, part)
        for others in sooner:
            rows += others[:, part]
        out[:, part] = rows


def gather(place, blocks, cap, sooner, after):
    arrays = arrays_of(blocks)
    rows, features = place.shape[0], arrays[0].shape[1]
    return call(
        functools.partial(gather_body, len(arrays), spots_of(blocks, arrays), cap),
        "gather",
        (place, *arrays, *sooner),
        [VMEM] * (1 + len(arrays) + len(sooner)),
        [jax.ShapeDtypeStruct((rows, features), BF16)],
        [VMEM],
        16,
        after=after,
    )[0]


def finish_body(count, spots, cap, place, sooner, *refs):
    arrays, out, whole, sems = refs[:count], *refs[count:]
    copies = []
    for i, part in enumerate(tiles(out.shape[1])):
        whole[:, part] = rows_of(place, arrays, spots, cap, part) + sooner[:, part]
        copies.append(pltpu.make_async_copy(whole.at[:, part], out.at[:, part], sems.at[i]))
        copies[-1].start()
    for copy in copies:
        copy.wait()


def finish(place, blocks, cap, sooner, after):
    arrays, (rows, features) = arrays_of(blocks), sooner.shape
    return call(
        functools.partial(finish_body, len(arrays), spots_of(blocks, arrays), cap),
        "finish",
        (place, sooner, *arrays),
        [VMEM] * (2 + len(arrays)),
        [jax.ShapeDtypeStruct((rows, features), BF16)],
        [HBM],
        16,
        [
            pltpu.VMEM((rows, features), BF16),
            pltpu.SemaphoreType.DMA((len(tiles(features)),)),
        ],
        after=after,
    )[0]


def swap(block, axis, k):
    size = lax.axis_size(axis)
    return lax.ppermute(block, axis, [(i, i ^ k) for i in range(size)])


def near_device(dy_values, dy_scales, expert_ids, saved_pre, w_gate, w_up, w_down):
    groups = lax.axis_size("expert")
    cap = saved_pre.shape[0] // groups
    features = dy_values.shape[1]
    keeps, gots, owns, others, returned, result = {}, {}, {}, {}, {}, {}

    place = find_place(expert_ids, groups, cap)
    last, sooner = [place], []
    scaled, crossing, ahead = pack(place, dy_values, dy_scales, ((1, 7), (6,)), cap)
    side = swap(crossing, "expert", 1)
    rest = pack_rest(place, scaled, [(k,) for k in LATER], cap, [crossing])
    last[:] = rest[-1:]
    blocks = {1: (side, 0)}
    for k, block in zip(LATER, rest):
        blocks[k] = (swap(block, "expert", k) if k else block, 0)

    def do_diagonal(_):
        both = pair([(ahead, 0), (side, cap)], cap, last)
        last[:] = [both]
        got = swap(both, "expert", 6)
        blocks.update({6: (got, 0), 7: (got, cap)})

    def do_first(c):
        send, keeps[c] = first([blocks[k] for k in CHUNKS[c]], w_down[0], cap, last)
        last[:] = [send]
        gots[c] = [swap(send, "dp", 1)]

    def do_add(c):
        part = add(keeps[c], gots[c], last)
        last[:] = [part]
        if len(gots[c]) == 1:
            gots[c].append(swap(part, "dp", 2))
        elif c in HELD:
            owns[c] = part
        else:
            owns[c], others[c] = part, swap(part, "dp", 1)

    def do_release(c):
        owns[c] = release(owns[c], last)
        last[:] = [owns[c]]
        others[c] = swap(owns[c], "dp", 1)

    def do_prep(_):
        *result["factors"], result["hidden"] = prep(saved_pre, last)
        last[:] = [result["hidden"]]

    def do_turn(_):
        turned = turn((w_gate[0], w_up[0]), place, PARTS, cap, last)
        result["weights"], result["places"] = turned[:2], turned[2:]
        last[:] = turned[:1]

    def do_second(c):
        chunk = CHUNKS[c]
        grads = second(
            owns[c], others[c], result["factors"], result["weights"], chunk, cap, 6 in chunk, last
        )
        last[:] = [grads[0]]
        if 6 in chunk:
            result["back"] = swap(grads[0], "expert", 6)
            returned[6] = (result["back"], 0)
        elif 0 in chunk:
            returned[0], result["near"] = (grads[0], 0), grads[1]
        else:
            returned.update({k: (swap(grad, "expert", k), 0) for k, grad in zip(chunk, grads)})

    def do_cross(_):
        both = pair([(result["near"], 0), (result["back"], cap)], cap, last)
        last[:] = [both]
        got = swap(both, "expert", 1)
        returned.update({1: (got, 0), 7: (got, cap)})

    def do_down(_):
        every = [blocks[k] for k in range(groups)]
        result["down"], flag = down(every, result["hidden"], features, last)
        last[:] = [flag]

    def do_gather(part):
        came = [returned[k] for k in PARTS[part]]
        sooner[:] = [gather(result["places"][part], came, cap, sooner, last)]
        last[:] = sooner

    steps = {
        "first": do_first,
        "add": do_add,
        "release": do_release,
        "diagonal": do_diagonal,
        "cross": do_cross,
        "prep": do_prep,
        "turn": do_turn,
        "second": do_second,
        "down": do_down,
        "gather": do_gather,
    }
    for step, c in ORDER:
        steps[step](c)
    came = [returned[k] for k in PARTS[-1]]
    grad_input = finish(result["places"][-1], came, cap, sooner[0], last)
    return (grad_input, result["down"][None])


def far_device(dy_values, dy_scales, expert_ids, saved_pre, w_gate, w_up, w_down):
    groups, width = lax.axis_size("expert"), w_down.shape[2]
    slots = saved_pre.shape[0]
    cap = slots // groups
    route = expert_ids[:, 0]
    rows, count = route.shape[0], dy_scales.shape[1]
    onehot = (route[:, None] == jnp.arange(groups, dtype=jnp.int32)[None, :]).astype(BF16)
    earlier = jnp.dot(jnp.tri(rows, k=-1, dtype=BF16), onehot, preferred_element_type=F32)
    rank = jnp.sum(earlier * onehot.astype(F32), axis=1).astype(jnp.int32)
    place = route * cap + rank
    chosen = (place[:, None] == jnp.arange(slots, dtype=jnp.int32)[None, :]).astype(BF16)
    scaled = dy_values.astype(F32).reshape(rows, count, -1) * dy_scales.astype(F32)[:, :, None]
    scaled = scaled.reshape(dy_values.shape).astype(BF16)
    packed = lax.dot_general(chosen, scaled, BY_ROWS, preferred_element_type=F32).astype(BF16)
    received = lax.all_to_all(packed, "expert", split_axis=0, concat_axis=0, tiled=True)
    gate, up, sigmoid = swish_parts(saved_pre, width)
    hidden = (gate * sigmoid * up).astype(BF16)
    partial = jnp.dot(received, w_down[0], preferred_element_type=F32)
    grad = lax.psum(partial, "dp")
    d_gate = (grad * up * sigmoid * (1.0 + gate * (1.0 - sigmoid))).astype(BF16)
    d_up = (grad * (gate * sigmoid)).astype(BF16)
    result = lax.dot_general(d_gate, w_gate[0], TRANSPOSED, preferred_element_type=F32)
    result += lax.dot_general(d_up, w_up[0], TRANSPOSED, preferred_element_type=F32)
    returned = lax.all_to_all(
        result.astype(BF16), "expert", split_axis=0, concat_axis=0, tiled=True
    )
    grad_input = jnp.dot(chosen, returned, preferred_element_type=F32).astype(BF16)
    grad_down = lax.dot_general(received, hidden, BY_ROWS, preferred_element_type=F32)
    return (grad_input, grad_down[None])


def solution(mesh):
    near = mesh.shape["expert"] == 8 and mesh.shape["dp"] == 4
    return jax.shard_map(
        near_device if near else far_device,
        mesh=mesh,
        in_specs=(
            P("expert", "dp"),
            P("expert", "dp"),
            P("expert", None),
            P("expert", None),
            P("expert", "dp", None),
            P("expert", "dp", None),
            P("expert", "dp", None),
        ),
        out_specs=(P("expert", "dp"), P("expert", "dp", None)),
        check_vma=False,
    )
```

```python
import functools

import jax
import jax.numpy as jnp
from jax import lax
from jax.experimental import pallas as pl
from jax.experimental.pallas import tpu as pltpu
from jax.sharding import PartitionSpec as P

CHUNKS = ((0, 1), (6, 7), (2, 4), (3, 5))
LATER = (2, 4, 3, 5, 0)
PARTS = (CHUNKS[2], CHUNKS[0] + CHUNKS[1], CHUNKS[3])
ORDER = (
    ("first", 0), ("diagonal", 0), ("add", 0), ("prep", 0), ("turn", 0), ("first", 1),
    ("first", 2), ("add", 0), ("add", 1), ("first", 3), ("add", 2), ("release", 0), ("add", 1),
    ("add", 3), ("down", 0), ("add", 2), ("second", 1), ("add", 3), ("second", 2), ("second", 0),
    ("second", 3), ("cross", 0), ("gather", 0), ("gather", 1),
)
HELD = (0,)
COST = {
    "place": 10**10, "pack": 10**10, "rest": 1, "first": 1, "prep": 1, "turn": 1,
    "add": 10**9, "release": 1, "pair": 1, "second": 10**10, "down": 1, "gather": 5 * 10**9, "finish": 1,
}
MIB = 1 << 20
BF16, F32 = jnp.bfloat16, jnp.float32
TRANSPOSED = (((1,), (1,)), ((), ()))
BY_ROWS = (((0,), (0,)), ((), ()))


VMEM, HBM, ANY = (
    pl.BlockSpec(memory_space=space) for space in (pltpu.VMEM, pltpu.HBM, pl.ANY)
)


def call(body, name, operands, specs, outs, out_specs, vmem=16, scratch=(), after=()):
    count, waits = len(operands), len(after)

    def run(*refs):
        body(*refs[:count], *refs[count + waits :])

    return pl.pallas_call(
        run,
        name=name,
        out_shape=outs,
        in_specs=list(specs) + [ANY] * waits,
        out_specs=out_specs,
        scratch_shapes=scratch,
        compiler_params=pltpu.CompilerParams(vmem_limit_bytes=vmem * MIB),
        cost_estimate=pl.CostEstimate(flops=COST[name], bytes_accessed=0, transcendentals=0),
    )(*operands, *after)


def in_hbm(array):
    return pltpu.with_memory_space_constraint(array, pltpu.HBM)


def swish_parts(pre, width):
    gate, up = pre[:, :width].astype(F32), pre[:, width:].astype(F32)
    sigmoid = jax.nn.sigmoid(gate)
    return gate, up, sigmoid


def tiles(size):
    step = 256 if size % 256 == 0 else size
    return [slice(i, i + step) for i in range(0, size, step)]


def arrays_of(blocks):
    found = []
    for array, _ in blocks:
        if not any(array is other for other in found):
            found.append(array)
    return found


def spots_of(blocks, arrays):
    return [(next(i for i, x in enumerate(arrays) if x is array), row) for array, row in blocks]


def rows_at(refs, spots, cap):
    return jnp.concatenate([refs[i][row : row + cap] for i, row in spots], axis=0)


def place_body(groups, cap, ids, place, ids_in, sems):
    bring = pltpu.make_async_copy(ids, ids_in, sems.at[0])
    bring.start()
    rows, slots, lines = ids.shape[1], groups * cap, max(8, groups)
    line = lax.broadcasted_iota(jnp.int32, (lines, rows), 0)
    sooner = lax.broadcasted_iota(jnp.int32, (rows, rows), 0)
    later = lax.broadcasted_iota(jnp.int32, (rows, rows), 1)
    before = jnp.where(sooner < later, 1.0, 0.0).astype(BF16)
    bring.wait()
    route = ids_in[...]
    onehot = jnp.where(line == route, 1.0, 0.0)
    earlier = jnp.dot(onehot.astype(BF16), before, preferred_element_type=F32)
    rank = jnp.sum(earlier * onehot, axis=0, keepdims=True).astype(jnp.int32)
    position = (route ^ lax.axis_index("expert")) * cap + rank
    slot = lax.broadcasted_iota(jnp.int32, (slots, rows), 0)
    place[...] = jnp.where(slot == position, 1.0, 0.0).astype(BF16)


def find_place(ids, groups, cap):
    rows = ids.shape[0]
    return call(
        functools.partial(place_body, groups, cap),
        "place",
        (in_hbm(ids.T),),
        (HBM,),
        [jax.ShapeDtypeStruct((groups * cap, rows), BF16)],
        [VMEM],
        16,
        [pltpu.VMEM((1, rows), jnp.int32), pltpu.SemaphoreType.DMA((1,))],
    )[0]


def put_blocks(place, rows, outs, groups, cap):
    chosen = rows_at([place], [(0, k * cap) for group in groups for k in group], cap)
    for part in tiles(rows.shape[1]):
        packed = jnp.dot(chosen, rows[:, part], preferred_element_type=F32).astype(BF16)
        start = 0
        for group, out in zip(groups, outs):
            out[:, part] = packed[start : start + len(group) * cap]
            start += len(group) * cap


def pack_body(groups, cap, place, scales, values, scaled, *outs):
    features, count = values.shape[1], scales.shape[0]
    owner = lax.broadcasted_iota(jnp.int32, (count, features), 1) // (features // count)
    spread = jnp.where(owner == lax.broadcasted_iota(jnp.int32, (count, features), 0), 1.0, 0.0)
    spread = spread.astype(BF16)
    for part in tiles(features):
        factor = lax.dot_general(
            scales[...], spread[:, part], BY_ROWS, preferred_element_type=F32
        )
        scaled[:, part] = (values[:, part].astype(F32) * factor).astype(BF16)
    put_blocks(place, scaled, outs, groups, cap)


def rest_body(groups, cap, place, scaled, *outs):
    put_blocks(place, scaled, outs, groups, cap)


def pack(place, values, scales, groups, cap):
    rows, features = values.shape
    return call(
        functools.partial(pack_body, groups, cap),
        "pack",
        (place, scales.T, values),
        [VMEM] * 3,
        [jax.ShapeDtypeStruct((rows, features), BF16)]
        + [jax.ShapeDtypeStruct((len(group) * cap, features), BF16) for group in groups],
        [VMEM] * (1 + len(groups)),
    )


def pack_rest(place, scaled, groups, cap, after):
    features = scaled.shape[1]
    return call(
        functools.partial(rest_body, groups, cap),
        "rest",
        (place, scaled),
        [VMEM] * 2,
        [jax.ShapeDtypeStruct((len(group) * cap, features), BF16) for group in groups],
        [VMEM] * len(groups),
        after=after,
    )


def pair_body(count, spots, cap, *refs):
    refs[count][...] = rows_at(refs[:count], spots, cap)


def pair(blocks, cap, after):
    arrays = arrays_of(blocks)
    shape = jax.ShapeDtypeStruct((len(blocks) * cap, arrays[0].shape[1]), BF16)
    return call(
        functools.partial(pair_body, len(arrays), spots_of(blocks, arrays), cap),
        "pair",
        arrays,
        [VMEM] * len(arrays),
        [shape],
        [VMEM],
        after=after,
    )[0]


def first_body(count, spots, cap, weight, *refs):
    arrays, send, keep, both = refs[:count], *refs[count:]
    rows = rows_at(arrays, spots, cap)
    width = weight.shape[1]
    for part in tiles(width):
        both[:, part] = jnp.dot(rows, weight[:, part], preferred_element_type=F32)
    halves = [slice(0, width // 2), slice(width // 2, width)]
    for odd, (theirs, mine) in enumerate((reversed(halves), halves)):

        @pl.when(lax.axis_index("dp") % 2 == odd)
        def _():
            send[...] = both[:, theirs].astype(BF16)
            keep[...] = both[:, mine]


def first(blocks, weight, cap, after):
    arrays = arrays_of(blocks)
    features, width = weight.shape
    size = len(blocks) * cap
    return call(
        functools.partial(first_body, len(arrays), spots_of(blocks, arrays), cap),
        "first",
        (weight, *arrays),
        [VMEM] * (1 + len(arrays)),
        [jax.ShapeDtypeStruct((size, width // 2), dtype) for dtype in (BF16, F32)],
        [VMEM] * 2,
        16,
        [pltpu.VMEM((size, width), F32)],
        after=after,
    )


def add_body(count, keep, *refs):
    total = keep[...]
    for got in refs[:count]:
        total = total + got[...].astype(F32)
    refs[count][...] = total.astype(BF16)


def add(keep, gots, after):
    return call(
        functools.partial(add_body, len(gots)),
        "add",
        (keep, *gots),
        [VMEM] * (1 + len(gots)),
        [jax.ShapeDtypeStruct(keep.shape, BF16)],
        [VMEM],
        16,
        after=after,
    )[0]


def release_body(total, out):
    out[...] = total[...]


def release(total, after):
    shape = jax.ShapeDtypeStruct(total.shape, total.dtype)
    return call(release_body, "release", (total,), [VMEM], [shape], [VMEM], after=after)[0]


def prep_body(saved, gate_factor, up_factor, hidden):
    slots, width = hidden.shape
    step = 32 if slots % 32 == 0 else slots

    def some(i, carry):
        at = pl.ds(pl.multiple_of(i * step, step), step)
        gate, up, sigmoid = swish_parts(saved[at, :], width)
        silu = gate * sigmoid
        gate_factor[at, :] = up * sigmoid * (1.0 + gate * (1.0 - sigmoid))
        up_factor[at, :] = silu
        hidden[at, :] = (silu * up).astype(BF16)
        return carry

    lax.fori_loop(0, slots // step, some, 0)


def prep(saved_pre, after):
    slots, width = saved_pre.shape[0], saved_pre.shape[1] // 2
    return call(
        prep_body,
        "prep",
        (saved_pre,),
        [VMEM],
        [jax.ShapeDtypeStruct((slots, width), dtype) for dtype in (F32, F32, BF16)],
        [VMEM] * 3,
        16,
        after=after,
    )


def turn_body(count, cap, groups, place, *refs):
    weights, turned, places = refs[:count], refs[count : 2 * count], refs[2 * count :]
    for weight, out in zip(weights, turned):
        for part in tiles(weight.shape[0]):
            out[:, part] = weight[part, :].T
    for group, out in zip(groups, places):
        out[...] = rows_at([place], [(0, k * cap) for k in group], cap).T


def turn(weights, place, groups, cap, after):
    count, rows = len(weights), place.shape[1]
    return call(
        functools.partial(turn_body, count, cap, groups),
        "turn",
        (place, *weights),
        [VMEM] * (1 + count),
        [jax.ShapeDtypeStruct(x.shape[::-1], x.dtype) for x in weights]
        + [jax.ShapeDtypeStruct((rows, len(group) * cap), BF16) for group in groups],
        [VMEM] * (count + len(groups)),
        16,
        after=after,
    )


def slots_of(ref, k, cap):
    start = pl.multiple_of((lax.axis_index("expert") ^ k) * cap, cap)
    return ref[pl.ds(start, cap), :]


def second_body(chunk, cap, own, other, gate_factor, up_factor, w_gate, w_up, *refs):
    outs, grads = refs[:-1], refs[-1]
    width, features = w_gate.shape
    halves = [slice(0, width // 2), slice(width // 2, width)]
    for odd, (theirs, mine) in enumerate((reversed(halves), halves)):

        @pl.when(lax.axis_index("dp") % 2 == odd)
        def _():
            grads[:, mine] = own[...]
            grads[:, theirs] = other[...]

    grad = grads[...].astype(F32)
    d_gate, d_up = (
        (grad * jnp.concatenate([slots_of(factor, k, cap) for k in chunk], axis=0))
        .astype(BF16)
        for factor in (gate_factor, up_factor)
    )
    for part in tiles(features):
        result = jnp.dot(d_gate, w_gate[:, part], preferred_element_type=F32)
        result += jnp.dot(d_up, w_up[:, part], preferred_element_type=F32)
        result = result.astype(BF16)
        size = result.shape[0] // len(outs)
        for i, out in enumerate(outs):
            out[:, part] = result[i * size : (i + 1) * size]


def second(own, other, factors, weights, chunk, cap, together, after):
    width, features = weights[0].shape
    count = 1 if together else len(chunk)
    size = len(chunk) // count * cap
    return call(
        functools.partial(second_body, chunk, cap),
        "second",
        (own, other, *factors, *weights),
        [VMEM] * 6,
        [jax.ShapeDtypeStruct((size, features), BF16)] * count,
        [VMEM] * count,
        24,
        [pltpu.VMEM((len(chunk) * cap, width), BF16)],
        after=after,
    )


def down_body(count, spots, hidden, *refs):
    arrays, out, flag, sums, sems = refs[:count], *refs[count:]
    flag[...] = jnp.zeros_like(flag)
    cap = hidden.shape[0] // len(spots)
    features, width = out.shape
    mine = jnp.concatenate([slots_of(hidden, k, cap) for k in range(len(spots))], axis=0)
    tile = sums.shape[1]
    copies = []
    for i in range(features // tile):
        part = [arrays[a][row : row + cap, i * tile : (i + 1) * tile] for a, row in spots]
        part = jnp.concatenate(part, axis=0)
        sums[i] = lax.dot_general(part, mine, BY_ROWS, preferred_element_type=F32)
        copies.append(
            pltpu.make_async_copy(sums.at[i], out.at[pl.ds(i * tile, tile)], sems.at[i])
        )
        copies[-1].start()
    for copy in copies:
        copy.wait()


def down(blocks, hidden, features, after):
    arrays = arrays_of(blocks)
    slots, width = hidden.shape
    tile = min(features, 256)
    steps = features // tile
    return call(
        functools.partial(down_body, len(arrays), spots_of(blocks, arrays)),
        "down",
        (hidden, *arrays),
        [VMEM] * (1 + len(arrays)),
        [jax.ShapeDtypeStruct((features, width), F32), jax.ShapeDtypeStruct((8, 128), F32)],
        [HBM, VMEM],
        24,
        [pltpu.VMEM((steps, tile, width), F32), pltpu.SemaphoreType.DMA((steps,))],
        after=after,
    )


def rows_of(place, arrays, spots, cap, part):
    returned = [arrays[i][row : row + cap, part] for i, row in spots]
    returned = jnp.concatenate(returned, axis=0)
    return jnp.dot(place[...], returned, preferred_element_type=F32).astype(BF16)


def gather_body(count, spots, cap, place, *refs):
    arrays, sooner, out = refs[:count], refs[count:-1], refs[-1]
    for part in tiles(out.shape[1]):
        rows = rows_of(place, arrays, spots, cap, part)
        for others in sooner:
            rows += others[:, part]
        out[:, part] = rows


def gather(place, blocks, cap, sooner, after):
    arrays = arrays_of(blocks)
    rows, features = place.shape[0], arrays[0].shape[1]
    return call(
        functools.partial(gather_body, len(arrays), spots_of(blocks, arrays), cap),
        "gather",
        (place, *arrays, *sooner),
        [VMEM] * (1 + len(arrays) + len(sooner)),
        [jax.ShapeDtypeStruct((rows, features), BF16)],
        [VMEM],
        16,
        after=after,
    )[0]


def finish_body(count, spots, cap, place, sooner, *refs):
    arrays, out, whole, sems = refs[:count], *refs[count:]
    copies = []
    for i, part in enumerate(tiles(out.shape[1])):
        whole[:, part] = rows_of(place, arrays, spots, cap, part) + sooner[:, part]
        copies.append(pltpu.make_async_copy(whole.at[:, part], out.at[:, part], sems.at[i]))
        copies[-1].start()
    for copy in copies:
        copy.wait()


def finish(place, blocks, cap, sooner, after):
    arrays, (rows, features) = arrays_of(blocks), sooner.shape
    return call(
        functools.partial(finish_body, len(arrays), spots_of(blocks, arrays), cap),
        "finish",
        (place, sooner, *arrays),
        [VMEM] * (2 + len(arrays)),
        [jax.ShapeDtypeStruct((rows, features), BF16)],
        [HBM],
        16,
        [
            pltpu.VMEM((rows, features), BF16),
            pltpu.SemaphoreType.DMA((len(tiles(features)),)),
        ],
        after=after,
    )[0]


def swap(block, axis, k):
    size = lax.axis_size(axis)
    return lax.ppermute(block, axis, [(i, i ^ k) for i in range(size)])


def near_device(dy_values, dy_scales, expert_ids, saved_pre, w_gate, w_up, w_down):
    groups = lax.axis_size("expert")
    cap = saved_pre.shape[0] // groups
    features = dy_values.shape[1]
    keeps, gots, owns, others, returned, result = {}, {}, {}, {}, {}, {}

    place = find_place(expert_ids, groups, cap)
    last, sooner = [place], []
    scaled, crossing, ahead = pack(place, dy_values, dy_scales, ((1, 7), (6,)), cap)
    side = swap(crossing, "expert", 1)
    rest = pack_rest(place, scaled, [(k,) for k in LATER], cap, [crossing])
    last[:] = rest[-1:]
    blocks = {1: (side, 0)}
    for k, block in zip(LATER, rest):
        blocks[k] = (swap(block, "expert", k) if k else block, 0)

    def do_diagonal(_):
        both = pair([(ahead, 0), (side, cap)], cap, last)
        last[:] = [both]
        got = swap(both, "expert", 6)
        blocks.update({6: (got, 0), 7: (got, cap)})

    def do_first(c):
        send, keeps[c] = first([blocks[k] for k in CHUNKS[c]], w_down[0], cap, last)
        last[:] = [send]
        gots[c] = [swap(send, "dp", 1)]

    def do_add(c):
        part = add(keeps[c], gots[c], last)
        last[:] = [part]
        if len(gots[c]) == 1:
            gots[c].append(swap(part, "dp", 2))
        elif c in HELD:
            owns[c] = part
        else:
            owns[c], others[c] = part, swap(part, "dp", 1)

    def do_release(c):
        owns[c] = release(owns[c], last)
        last[:] = [owns[c]]
        others[c] = swap(owns[c], "dp", 1)

    def do_prep(_):
        *result["factors"], result["hidden"] = prep(saved_pre, last)
        last[:] = [result["hidden"]]

    def do_turn(_):
        turned = turn((w_gate[0], w_up[0]), place, PARTS, cap, last)
        result["weights"], result["places"] = turned[:2], turned[2:]
        last[:] = turned[:1]

    def do_second(c):
        chunk = CHUNKS[c]
        grads = second(
            owns[c], others[c], result["factors"], result["weights"], chunk, cap, 6 in chunk, last
        )
        last[:] = [grads[0]]
        if 6 in chunk:
            result["back"] = swap(grads[0], "expert", 6)
            returned[6] = (result["back"], 0)
        elif 0 in chunk:
            returned[0], result["near"] = (grads[0], 0), grads[1]
        else:
            returned.update({k: (swap(grad, "expert", k), 0) for k, grad in zip(chunk, grads)})

    def do_cross(_):
        both = pair([(result["near"], 0), (result["back"], cap)], cap, last)
        last[:] = [both]
        got = swap(both, "expert", 1)
        returned.update({1: (got, 0), 7: (got, cap)})

    def do_down(_):
        every = [blocks[k] for k in range(groups)]
        result["down"], flag = down(every, result["hidden"], features, last)
        last[:] = [flag]

    def do_gather(part):
        came = [returned[k] for k in PARTS[part]]
        sooner[:] = [gather(result["places"][part], came, cap, sooner, last)]
        last[:] = sooner

    steps = {
        "first": do_first,
        "add": do_add,
        "release": do_release,
        "diagonal": do_diagonal,
        "cross": do_cross,
        "prep": do_prep,
        "turn": do_turn,
        "second": do_second,
        "down": do_down,
        "gather": do_gather,
    }
    for step, c in ORDER:
        steps[step](c)
    came = [returned[k] for k in PARTS[-1]]
    grad_input = finish(result["places"][-1], came, cap, sooner[0], last)
    return (grad_input, result["down"][None])


def far_device(dy_values, dy_scales, expert_ids, saved_pre, w_gate, w_up, w_down):
    groups, width = lax.axis_size("expert"), w_down.shape[2]
    slots = saved_pre.shape[0]
    cap = slots // groups
    route = expert_ids[:, 0]
    rows, count = route.shape[0], dy_scales.shape[1]
    onehot = (route[:, None] == jnp.arange(groups, dtype=jnp.int32)[None, :]).astype(BF16)
    earlier = jnp.dot(jnp.tri(rows, k=-1, dtype=BF16), onehot, preferred_element_type=F32)
    rank = jnp.sum(earlier * onehot.astype(F32), axis=1).astype(jnp.int32)
    place = route * cap + rank
    chosen = (place[:, None] == jnp.arange(slots, dtype=jnp.int32)[None, :]).astype(BF16)
    scaled = dy_values.astype(F32).reshape(rows, count, -1) * dy_scales.astype(F32)[:, :, None]
    scaled = scaled.reshape(dy_values.shape).astype(BF16)
    packed = lax.dot_general(chosen, scaled, BY_ROWS, preferred_element_type=F32).astype(BF16)
    received = lax.all_to_all(packed, "expert", split_axis=0, concat_axis=0, tiled=True)
    gate, up, sigmoid = swish_parts(saved_pre, width)
    hidden = (gate * sigmoid * up).astype(BF16)
    partial = jnp.dot(received, w_down[0], preferred_element_type=F32)
    grad = lax.psum(partial, "dp")
    d_gate = (grad * up * sigmoid * (1.0 + gate * (1.0 - sigmoid))).astype(BF16)
    d_up = (grad * (gate * sigmoid)).astype(BF16)
    result = lax.dot_general(d_gate, w_gate[0], TRANSPOSED, preferred_element_type=F32)
    result += lax.dot_general(d_up, w_up[0], TRANSPOSED, preferred_element_type=F32)
    returned = lax.all_to_all(
        result.astype(BF16), "expert", split_axis=0, concat_axis=0, tiled=True
    )
    grad_input = jnp.dot(chosen, returned, preferred_element_type=F32).astype(BF16)
    grad_down = lax.dot_general(received, hidden, BY_ROWS, preferred_element_type=F32)
    return (grad_input, grad_down[None])


def solution(mesh):
    near = mesh.shape["expert"] == 8 and mesh.shape["dp"] == 4
    return jax.shard_map(
        near_device if near else far_device,
        mesh=mesh,
        in_specs=(
            P("expert", "dp"),
            P("expert", "dp"),
            P("expert", None),
            P("expert", None),
            P("expert", "dp", None),
            P("expert", "dp", None),
            P("expert", "dp", None),
        ),
        out_specs=(P("expert", "dp"), P("expert", "dp", None)),
        check_vma=False,
    )
```
